256 devices in a mesh: dp: 64 (over z, x, core), tensor: 4 (over y).
Axes of the slice: x: 4, y: 4, z: 8, core: 2. Of those that a mesh axis runs over, the one named last changes fastest.
Arguments:
- tokens: bfloat16 [8192, 4096], P(('dp', 'tensor')), may hold values from -6 to 6
- query_base_weight: bfloat16 [4096, 4096], P(None, 'tensor'), may hold values from -0.09375 to 0.09375
- adapter_down_weight: bfloat16 [64, 16, 4096], P('dp', None, 'tensor'), may hold values from -0.09375 to 0.09375
- adapter_up_weight: bfloat16 [64, 16, 4096], P('dp', None, 'tensor'), may hold values from -0.375 to 0.375
- upstream: bfloat16 [8192, 4096], P('dp', 'tensor'), may hold values from -6 to 6
- adapter_per_block: int32 [64, 1], P('dp'), may hold values from 0 to 63
- owner: int32 [64], replicated, may hold values from 0 to 63, each once
Outputs:
- mixed: bfloat16 [8192, 4096], P('dp', 'tensor')
- input_gradient: bfloat16 [8192, 4096], P(('dp', 'tensor'))
- down_gradient: float32 [64, 16, 4096], P('dp', None, 'tensor')
- up_gradient: float32 [64, 16, 4096], P('dp', None, 'tensor')
The draws below stay inside these ranges and needn't reach their ends.
Inputs may be any that keep to these rules, and one draw needn't show every extreme that they name: `adapter_per_block`: every adapter has at least one block. `owner`: each slot is taken by exactly one adapter.
All inputs are finite; a program needn't handle non-finite values.
Results may differ from the reference program's by a relative error of at most 0.0032.
Values may be sent and summed in bfloat16 or wider, within the bound.
A program may use at most 128 MiB of HBM per device.

```python
import jax
import jax.numpy as jnp
from jax import lax

MODEL_WIDTH = 4096
ADAPTER_RANK = 16
BLOCK = 128
ADAPTER_TOTAL = 64
BLOCKS = 64
TOKENS = 8192


def level_of(rng, shape, cuts, low, top_value):
    level = 1.0
    for dim, shards_of in cuts:
        steps = jax.random.uniform(jax.random.fold_in(jax.random.fold_in(rng, 6), dim), (shards_of,), jnp.float32, low / len(cuts), top_value / len(cuts))
        level = level * jnp.repeat(jnp.exp(steps), shape[dim] // shards_of).reshape((-1,) + (1,) * (len(shape) - 1 - dim))
    return level


def choose_distinct(stream_key, rows, count, top, lift):
    ranking = jax.random.permutation(jax.random.fold_in(stream_key, 1), count)
    favour = ranking
    for power in range(3):
        favour = favour * favour // count
    favour = favour * lift // count
    lots = jax.random.randint(jax.random.fold_in(stream_key, 2), (rows, count), 0, 4096) + favour
    sure = jax.random.permutation(jax.random.fold_in(stream_key, 3), rows)[jnp.arange(count) % rows]
    lots = jnp.where(jnp.arange(rows)[:, None] == sure[None, :], 1 << 14, lots)
    priority = lots * count + jnp.arange(count)
    return lax.top_k(priority.astype(jnp.int32), top)[1].astype(jnp.int32)


def centred(stream_key, extent, width, most, pieces=(), kind=jnp.bfloat16):
    level = level_of(stream_key, extent, pieces, -0.22, 0.18) if pieces else 1.0
    result = jax.random.normal(stream_key, extent, jnp.float32) * width * level
    return jnp.minimum(jnp.maximum(result, -most), most).astype(kind)


def setup_inputs(seed: int = 0) -> dict:
    key_list = jax.random.split(jax.random.key(seed), 8)
    return {
        "tokens": centred(key_list[0], (TOKENS, MODEL_WIDTH), 1.0, 6.0, ((0, 256),)),
        "query_base_weight": centred(key_list[1], (MODEL_WIDTH, MODEL_WIDTH), MODEL_WIDTH ** -0.5, 0.09375, ((1, 4),)),
        "adapter_down_weight": centred(key_list[2], (ADAPTER_TOTAL, ADAPTER_RANK, MODEL_WIDTH), MODEL_WIDTH ** -0.5, 0.09375, ((0, 64), (2, 4))),
        "adapter_up_weight": centred(key_list[3], (ADAPTER_TOTAL, ADAPTER_RANK, MODEL_WIDTH), (16 * ADAPTER_RANK) ** -0.5, 0.375, ((0, 64), (2, 4))),
        "upstream": centred(key_list[4], (TOKENS, MODEL_WIDTH), 1.0, 6.0, ((0, 64), (1, 4))),
        "adapter_per_block": choose_distinct(key_list[5], BLOCKS, ADAPTER_TOTAL, 1, 256),
        "owner": jax.random.permutation(key_list[6], ADAPTER_TOTAL).astype(jnp.int32),
    }


adapter_scale = 2.0


def reference(tokens, query_base_weight, adapter_down_weight, adapter_up_weight, upstream, adapter_per_block, owner):
    slot_indices = owner[adapter_per_block[:, 0]]
    down_chosen = adapter_down_weight[slot_indices].astype(jnp.float32)
    up_chosen = adapter_up_weight[slot_indices].astype(jnp.float32)
    token_blocks = tokens.reshape(-1, BLOCK, MODEL_WIDTH).astype(jnp.float32)
    backward_blocks = upstream.reshape(-1, BLOCK, MODEL_WIDTH).astype(jnp.float32)
    reduced_hidden = jnp.einsum('mtn,myn->mty', token_blocks, down_chosen).astype(jnp.bfloat16)
    reduced_backward = jnp.einsum('mtn,myn->mty', backward_blocks, up_chosen).astype(jnp.bfloat16)
    reduced_function = reduced_hidden.astype(jnp.float32)
    backward_function = reduced_backward.astype(jnp.float32)
    mixed = jnp.dot(tokens, query_base_weight, preferred_element_type=jnp.float32)
    mixed = mixed + adapter_scale * jnp.einsum('xzv,xva->xza', reduced_function, up_chosen).reshape(-1, MODEL_WIDTH)
    input_gradient = jnp.dot(upstream, query_base_weight.T, preferred_element_type=jnp.float32)
    input_gradient = input_gradient + adapter_scale * jnp.einsum('xzv,xva->xza', backward_function, down_chosen).reshape(-1, MODEL_WIDTH)
    down_contributions = adapter_scale * jnp.einsum('phl,phj->plj', backward_function, token_blocks)
    up_contributions = adapter_scale * jnp.einsum('phl,phj->plj', reduced_function, backward_blocks)
    down_gradient = jax.ops.segment_sum(down_contributions, slot_indices, num_segments=ADAPTER_TOTAL)
    up_gradient = jax.ops.segment_sum(up_contributions, slot_indices, num_segments=ADAPTER_TOTAL)
    return mixed.astype(jnp.bfloat16), input_gradient.astype(jnp.bfloat16), down_gradient, up_gradient
```

```python
import functools

import jax
import jax.numpy as jnp
from jax import lax
from jax.experimental import pallas as pl
from jax.experimental.pallas import tpu as pltpu
from jax.sharding import PartitionSpec as P

MESH = pl.DeviceIdType.MESH
SIDE = 8
RING = 4
RANK = 16
ITEM = 2 * RANK
LANE = 128
SLOTS = SIDE * SIDE
PARTS = SLOTS * 4

F32 = jnp.float32
BF16 = jnp.bfloat16


def dot(a, b):
    return jnp.dot(a, b, preferred_element_type=F32)


def dot_t(a, b):
    return lax.dot_general(a, b, (((1,), (1,)), ((), ())), preferred_element_type=F32)


def kernel(
    tokens, weight, down, up, upstream, adapter, owner,
    mixed_out, grad_out, down_out, up_out,
    w, tok, ups, part, send, relay_up, relay_dn, got_up, got_dn, mix, mix_b, rows_b,
    item, s1, r1, s2, r2, s3, r3, s4, r4, g1, h1, g2, h2, g3, h3, g4, h4,
    low_all, reorder, select, select_t, down_b, up_b,
    local_sem, out_sem, ag_s, ag_r, rs_s, rs_r, low_s, low_r, ph_s, ph_r,
):
    dp = lax.axis_index("dp")
    y = lax.axis_index("tensor")
    a, b = dp // SIDE, dp % SIDE
    rows = tokens.shape[0]
    cols = weight.shape[1]

    def ring(step):
        return (y + step) % RING

    def here(c):
        return pl.ds(pl.multiple_of(c * rows, rows), rows)

    def wide(c):
        return pl.ds(pl.multiple_of(c * cols, cols), cols)

    sent = []

    def push(src, dst, ssem, rsem, device):
        copy = pltpu.make_async_remote_copy(
            src_ref=src, dst_ref=dst, send_sem=ssem, recv_sem=rsem,
            device_id=device, device_id_type=MESH,
        )
        copy.start()
        sent.append(copy)
        return copy

    load_items = [
        pltpu.make_async_copy(down.at[0], item.at[pl.ds(0, RANK)], local_sem.at[0]),
        pltpu.make_async_copy(up.at[0], item.at[pl.ds(RANK, RANK)], local_sem.at[1]),
    ]
    order = (2, 1, 3, 0)
    load_tok = [
        pltpu.make_async_copy(
            tokens.at[:, wide(ring(k))], tok.at[ring(k), here(y)], local_sem.at[2 + k]
        )
        for k in range(RING)
    ]
    load_ups = pltpu.make_async_copy(upstream, ups, local_sem.at[6])
    load_w = [
        pltpu.make_async_copy(weight.at[wide(ring(k))], w.at[ring(k)], local_sem.at[7 + k])
        for k in range(RING)
    ]
    for copy in load_items:
        copy.start()
    for k in order:
        load_tok[k].start()
    load_ups.start()

    barrier = pltpu.get_barrier_semaphore()
    peers = [(dp, ring(k)) for k in range(1, RING)]
    peers += [(a * SIDE + (b + j) % SIDE, y) for j in range(1, SIDE)]
    peers += [((a + j) % SIDE * SIDE + b, y) for j in range(1, SIDE)]
    for device in peers:
        pl.semaphore_signal(barrier, inc=1, device_id=device, device_id_type=MESH)
    for k in (2, 3, 1, 0):
        load_w[k].start()

    row_id = lax.broadcasted_iota(jnp.int32, (PARTS, PARTS), 0)
    col_id = lax.broadcasted_iota(jnp.int32, (PARTS, PARTS), 1)
    flipped = (((row_id >> 2) & 7) << 5) | ((row_id >> 5) << 2) | (row_id & 3)
    reorder[...] = (col_id == flipped).astype(F32).astype(BF16)
    block_tag = jnp.full((RANK, LANE), adapter[0, 0], jnp.int32).astype(F32).astype(BF16)
    for copy in load_items:
        copy.wait()
    for k in range(SIDE):
        s1[k, 0:ITEM, :] = item[:, k * LANE:(k + 1) * LANE]
        s1[k, ITEM:, :] = block_tag
    r1[b] = s1[b]
    for k in order:
        load_tok[k].wait()

    pl.semaphore_wait(barrier, len(peers))

    up_dev, dn_dev = (dp, ring(1)), (dp, ring(3))

    def across(phase, src, dst):
        return [
            push(src.at[(b + j) % SIDE], dst.at[b], ph_s.at[phase, j], ph_r.at[phase, j],
                 (a * SIDE + (b + j) % SIDE, y))
            for j in range(1, SIDE)
        ]

    def along(phase, src, dst):
        return [
            push(src.at[(a + j) % SIDE], dst.at[a], ph_s.at[phase, j], ph_r.at[phase, j],
                 ((a + j) % SIDE * SIDE + b, y))
            for j in (4, 3, 5, 2, 6, 1, 7)
        ]

    def arrive(copies):
        for copy in copies:
            copy.wait_recv()

    def token_send(c, index, device):
        return push(tok.at[c, here(y)], tok.at[c, here(y)], ag_s.at[index], ag_r.at[index], device)

    def token_forward(c, owner_y, index, device):
        return push(tok.at[c, here(owner_y)], tok.at[c, here(owner_y)], ag_s.at[index], ag_r.at[index], device)

    ag_up = [token_send(ring(2), 0, up_dev)]
    ag_dn = [token_send(ring(3), 6, dn_dev)]
    first = across(0, s1, r1)
    ag_up.append(token_send(ring(1), 1, up_dev))
    ag_dn.append(token_send(ring(0), 7, dn_dev))
    ag_up.append(token_send(ring(3), 2, up_dev))
    ag_dn.append(token_send(ring(2), 8, dn_dev))
    ag_up.append(token_send(ring(0), 3, up_dev))
    ag_dn.append(token_send(ring(1), 9, dn_dev))

    def backward(k):
        c = ring(k)
        load_w[k].wait()
        if k == 2:
            load_ups.wait()
        part[c] = dot_t(ups[...], w[c])
        if k:
            send[c] = part[c].astype(BF16)

    backward(2)
    arrive(first)
    tags = r1[:, ITEM:, :].reshape(SIDE * RANK, LANE)
    tag_row = lax.broadcasted_iota(jnp.int32, (RANK, SIDE * RANK), 0)
    tag_col = lax.broadcasted_iota(jnp.int32, (RANK, SIDE * RANK), 1)
    pick = ((tag_col == (tag_row << 4)) & (tag_row < SIDE)).astype(F32).astype(BF16)
    row_tags = dot(pick, tags).astype(BF16)
    pieces = dot(reorder[...], r1[:, 0:ITEM, :].reshape(PARTS, LANE)).astype(BF16)
    s2[:, 0:ITEM, :] = pieces.reshape(SIDE, ITEM, LANE)
    for k in range(SIDE):
        s2[k, ITEM:, :] = row_tags
    r2[a] = s2[a]
    second = along(1, s2, r2)

    ag_up[0].wait_recv()
    ag_up.append(token_forward(ring(1), ring(3), 4, up_dev))
    ag_dn[0].wait_recv()
    ag_dn.append(token_forward(ring(0), ring(1), 10, dn_dev))
    backward(3)

    arrive(second)
    tags = r2[:, ITEM:, :].reshape(SIDE * RANK, LANE)
    part_row = lax.broadcasted_iota(jnp.int32, (PARTS, SIDE * RANK), 0)
    tag_col = lax.broadcasted_iota(jnp.int32, (PARTS, SIDE * RANK), 1)
    pick = (tag_col == (((part_row >> 5) << 4) | ((part_row >> 2) & 7))).astype(F32).astype(BF16)
    adapter_of = dot(pick, tags)[:, 0:SLOTS].astype(jnp.int32)
    lane = lax.broadcasted_iota(jnp.int32, (PARTS, SLOTS), 1)
    uses = (adapter_of == lane).astype(F32).astype(BF16)
    slot_row = lax.broadcasted_iota(jnp.int32, (PARTS, SLOTS), 0) >> 2
    owns = (owner[...] == slot_row).astype(F32).astype(BF16)
    same_part = ((row_id ^ col_id) & 3) == 0
    select[...] = jnp.where(same_part, dot_t(uses, owns), 0.0).astype(BF16)
    chosen_parts = dot(select[...], r2[:, 0:ITEM, :].reshape(PARTS, LANE)).astype(BF16)
    s3[...] = chosen_parts.reshape(SIDE, ITEM, LANE)
    r3[a] = s3[a]
    third = along(2, s3, r3)
    select_t[...] = jnp.where(same_part, dot_t(owns, uses), 0.0).astype(BF16)

    ag_up[1].wait_recv()
    ag_up.append(token_forward(ring(0), ring(3), 5, up_dev))
    ag_dn[1].wait_recv()
    ag_dn.append(token_forward(ring(1), ring(1), 11, dn_dev))
    backward(1)

    arrive(third)
    s4[...] = dot(reorder[...], r3[...].reshape(PARTS, LANE)).astype(BF16).reshape(SIDE, ITEM, LANE)
    r4[b] = s4[b]
    fourth = across(3, s4, r4)
    backward(0)

    def rows_send(c, to, dst, index, device):
        return push(send.at[c, here(to)], dst, rs_s.at[index], rs_r.at[index], device)

    far_up = [
        rows_send(ring(2), ring(2), relay_up.at[0], 0, up_dev),
        rows_send(ring(3), ring(2), relay_up.at[1], 1, up_dev),
    ]
    far_dn = [rows_send(ring(1), ring(2), relay_dn.at[0], 6, dn_dev)]
    near_up = [rows_send(ring(3), ring(1), got_up.at[ring(3)], 2, up_dev)]
    near_dn = [rows_send(ring(3), ring(3), got_dn.at[ring(3)], 8, dn_dev)]

    arrive(fourth)
    down_here = jnp.concatenate([r4[k, 0:RANK, :] for k in range(SIDE)], axis=1)
    up_here = jnp.concatenate([r4[k, RANK:, :] for k in range(SIDE)], axis=1)
    low_all[y, RANK:, :] = dot_t(up_here, ups[...])
    for copy in (ag_up[4],):
        copy.wait_recv()
    low_all[y, 0:RANK, :] = dot_t(down_here, tok[y])
    lows = [
        push(low_all.at[y], low_all.at[y], low_s.at[k - 1], low_r.at[k - 1], (dp, ring(k)))
        for k in range(1, RING)
    ]

    def relayed(c, to, relay, dst, index, device):
        send[c, here(to), :] = (part[c, here(to), :] + relay[...].astype(F32)).astype(BF16)
        return rows_send(c, to, dst, index, device)

    far_up[0].wait_recv()
    near_up.append(relayed(ring(1), ring(1), relay_up.at[0], got_up.at[ring(1)], 3, up_dev))
    far_dn[0].wait_recv()
    near_dn.append(relayed(ring(2), ring(3), relay_dn.at[0], got_dn.at[ring(2)], 9, dn_dev))
    far_up[1].wait_recv()
    near_up.append(relayed(ring(2), ring(1), relay_up.at[1], got_up.at[ring(2)], 4, up_dev))

    mix[...] = dot(tok[y], w[y])

    arrive(lows)
    total = low_all[0] + low_all[1] + low_all[2] + low_all[3]
    low_t = total[0:RANK].astype(BF16)
    back_t = total[RANK:].astype(BF16)
    flat = total.T
    low = flat[:, 0:RANK].astype(BF16)
    back = flat[:, RANK:].astype(BF16)

    down_term = (2.0 * dot(back_t, tok[y])).astype(BF16)
    up_term = (2.0 * dot(low_t, ups[...])).astype(BF16)
    for k in range(SIDE):
        g1[k, 0:RANK, :] = down_term[:, k * LANE:(k + 1) * LANE]
        g1[k, RANK:, :] = up_term[:, k * LANE:(k + 1) * LANE]
    h1[b] = g1[b]
    first = across(4, g1, h1)

    part[y] = part[y] + 2.0 * dot(back, down_here)
    send[y] = part[y].astype(BF16)
    far_dn.append(rows_send(y, ring(2), relay_dn.at[1], 7, dn_dev))
    near_up.append(rows_send(y, ring(1), got_up.at[y], 5, up_dev))
    near_dn.append(rows_send(y, ring(3), got_dn.at[y], 10, dn_dev))
    mix[...] += 2.0 * dot(low, up_here)

    arrive(first)
    g2[...] = dot(reorder[...], h1[...].reshape(PARTS, LANE)).astype(BF16).reshape(SIDE, ITEM, LANE)
    h2[a] = g2[a]
    second = along(5, g2, h2)

    ag_up[2].wait_recv()
    ag_up[3].wait_recv()
    ag_up[5].wait_recv()
    ag_dn[2].wait_recv()
    ag_dn[3].wait_recv()
    ag_dn[4].wait_recv()
    ag_dn[5].wait_recv()
    mix[...] += dot(tok[ring(1)], w[ring(1)])

    arrive(second)
    owned = dot(select_t[...], h2[...].reshape(PARTS, LANE)).astype(BF16)
    g3[...] = owned.reshape(SIDE, ITEM, LANE)
    h3[a] = g3[a]
    third = along(6, g3, h3)

    far_dn[1].wait_recv()
    near_dn.append(relayed(ring(1), ring(3), relay_dn.at[1], got_dn.at[ring(1)], 11, dn_dev))

    mix[...] += dot(tok[ring(3)], w[ring(3)])

    arrive(third)
    g4[...] = dot(reorder[...], h3[...].reshape(PARTS, LANE)).astype(BF16).reshape(SIDE, ITEM, LANE)
    h4[b] = g4[b]
    fourth = across(7, g4, h4)

    mix_b[...] = (mix[...] + dot(tok[ring(2)], w[ring(2)])).astype(BF16)
    outs = [pltpu.make_async_copy(mix_b, mixed_out, out_sem.at[0])]
    outs[0].start()

    arrive(fourth)
    for k in range(SIDE):
        down_b[:, k * LANE:(k + 1) * LANE] = h4[k, 0:RANK, :].astype(F32)
        up_b[:, k * LANE:(k + 1) * LANE] = h4[k, RANK:, :].astype(F32)
    outs.append(pltpu.make_async_copy(down_b, down_out.at[0], out_sem.at[1]))
    outs[-1].start()
    outs.append(pltpu.make_async_copy(up_b, up_out.at[0], out_sem.at[2]))
    outs[-1].start()

    arrive(near_up)
    arrive(near_dn)
    for k in range(RING):
        c = ring(k)
        rows_b[c] = (
            part[c, here(y), :] + got_up[c].astype(F32) + got_dn[c].astype(F32)
        ).astype(BF16)
        outs.append(pltpu.make_async_copy(rows_b.at[c], grad_out.at[:, wide(c)], out_sem.at[3 + k]))
        outs[-1].start()
    for copy in sent:
        copy.wait_send()
    for copy in outs:
        copy.wait()


def per_device(tokens, weight, down, up, upstream, adapter, owner):
    rows, width = tokens.shape
    block, cols = upstream.shape
    any_spec = pl.BlockSpec(memory_space=pl.ANY)
    small = lambda: pltpu.VMEM((SIDE, ITEM, LANE), BF16)
    tagged = lambda: pltpu.VMEM((SIDE, ITEM + RANK, LANE), BF16)
    dma = lambda *shape: pltpu.SemaphoreType.DMA(shape)
    scratch = [
        pltpu.VMEM((RING, cols, cols), BF16),
        pltpu.VMEM((RING, block, cols), BF16),
        pltpu.VMEM((block, cols), BF16),
        pltpu.VMEM((RING, block, cols), F32),
        pltpu.VMEM((RING, block, cols), BF16),
        pltpu.VMEM((2, rows, cols), BF16),
        pltpu.VMEM((2, rows, cols), BF16),
        pltpu.VMEM((RING, rows, cols), BF16),
        pltpu.VMEM((RING, rows, cols), BF16),
        pltpu.VMEM((block, cols), F32),
        pltpu.VMEM((block, cols), BF16),
        pltpu.VMEM((RING, rows, cols), BF16),
        pltpu.VMEM((ITEM, cols), BF16),
        tagged(), tagged(), tagged(), tagged(),
        small(), small(), small(), small(),
        small(), small(), small(), small(), small(), small(), small(), small(),
        pltpu.VMEM((RING, ITEM, block), F32),
        pltpu.VMEM((PARTS, PARTS), BF16),
        pltpu.VMEM((PARTS, PARTS), BF16),
        pltpu.VMEM((PARTS, PARTS), BF16),
        pltpu.VMEM((RANK, cols), F32),
        pltpu.VMEM((RANK, cols), F32),
        dma(11), dma(7), dma(12), dma(12), dma(12), dma(12), dma(3), dma(3),
        dma(8, SIDE), dma(8, SIDE),
    ]
    return pl.pallas_call(
        kernel,
        out_shape=(
            jax.ShapeDtypeStruct((block, cols), BF16),
            jax.ShapeDtypeStruct((rows, width), BF16),
            jax.ShapeDtypeStruct(down.shape, F32),
            jax.ShapeDtypeStruct(up.shape, F32),
        ),
        in_specs=[any_spec] * 5
        + [pl.BlockSpec(memory_space=pltpu.SMEM), pl.BlockSpec(memory_space=pltpu.VMEM)],
        out_specs=(any_spec,) * 4,
        scratch_shapes=scratch,
        compiler_params=pltpu.CompilerParams(
            collective_id=0, has_side_effects=True, vmem_limit_bytes=56 * 1024 * 1024
        ),
        cost_estimate=pl.CostEstimate(
            flops=4 * block * width * cols, bytes_accessed=12 * 1024 * 1024, transcendentals=0
        ),
    )(tokens, weight, down, up, upstream, adapter, owner.reshape(1, -1))


def solution(mesh):
    return jax.shard_map(
        per_device,
        mesh=mesh,
        in_specs=(
            P(("dp", "tensor"), None),
            P(None, "tensor"),
            P("dp", None, "tensor"),
            P("dp", None, "tensor"),
            P("dp", "tensor"),
            P("dp", None),
            P(),
        ),
        out_specs=(
            P("dp", "tensor"),
            P(("dp", "tensor"), None),
            P("dp", None, "tensor"),
            P("dp", None, "tensor"),
        ),
        check_vma=False,
    )
```

```python
import jax
import jax.numpy as jnp
from jax import lax
from jax.experimental import pallas as pl
from jax.experimental.pallas import tpu as pltpu
from jax.sharding import PartitionSpec as P

MESH = pl.DeviceIdType.MESH
DEEP = 8
WIDE = 4
CHIPS = DEEP * WIDE
RING = 4
RANK = 16
ITEM = 2 * RANK
TILE = 8
TAGGED = 2 * TILE
LANE = 128
FAR_FIRST = [
    (dz, dx) for dz in (4, 3, 5, 2, 6, 1, 7, 0) for dx in (2, 1, 3, 0) if dz or dx
]

F32 = jnp.float32
BF16 = jnp.bfloat16


def dot(a, b):
    return jnp.dot(a, b, preferred_element_type=F32)


def dot_t(a, b):
    return lax.dot_general(a, b, (((1,), (1,)), ((), ())), preferred_element_type=F32)


def one_hot(condition):
    return condition.astype(F32).astype(BF16)


def ids(rows, cols, dim):
    return lax.broadcasted_iota(jnp.int32, (rows, cols), dim)


def kernel(
    tokens, weight, down, up, upstream, adapter, owner,
    mixed_out, grad_out, down_out, up_out,
    w, tok, ups, part, send, relay_up, relay_dn, got_up, got_dn, mix,
    item, s1, r1, s3, r3, g1, h1, g3, h3, low_all, back_a, back_b,
    local_sem, ag_s, ag_r, rs_s, rs_r, low_s, low_r, ph_s, ph_r,
):
    dp = lax.axis_index("dp")
    y = lax.axis_index("tensor")
    chip, core = dp // 2, dp % 2
    other = 1 - core
    z, x = chip // WIDE, chip % WIDE
    z_at = [lax.rem(z + j, DEEP) for j in range(DEEP)]
    x_at = [lax.rem(x + j, WIDE) for j in range(WIDE)]
    rows = tokens.shape[0]
    cols = weight.shape[1]
    ring_at = [lax.rem(y + j, RING) for j in range(RING)]
    sibling = (chip * 2 + other, y)

    def ring(step):
        return ring_at[step]

    def here(c):
        return pl.ds(pl.multiple_of(c * rows, rows), rows)

    def wide(c):
        return pl.ds(pl.multiple_of(c * cols, cols), cols)

    sent = []

    def push(src, dst, ssem, rsem, device):
        copy = pltpu.make_async_remote_copy(
            src_ref=src, dst_ref=dst, send_sem=ssem, recv_sem=rsem,
            device_id=device, device_id_type=MESH,
        )
        copy.start()
        sent.append(copy)
        return copy

    load_items = [
        pltpu.make_async_copy(down.at[0], item.at[pl.ds(0, RANK)], local_sem.at[0]),
        pltpu.make_async_copy(up.at[0], item.at[pl.ds(RANK, RANK)], local_sem.at[1]),
    ]
    order = (2, 1, 3, 0)
    load_tok = [
        pltpu.make_async_copy(
            tokens.at[:, wide(ring(k))], tok.at[ring(k), here(y)], local_sem.at[2 + k]
        )
        for k in range(RING)
    ]
    load_ups = pltpu.make_async_copy(upstream, ups, local_sem.at[6])
    load_w = [
        pltpu.make_async_copy(weight.at[wide(ring(k))], w.at[ring(k)], local_sem.at[7 + k])
        for k in range(RING)
    ]
    for copy in load_items:
        copy.start()

    barrier = pltpu.get_barrier_semaphore()

    def chip_at(dz, dx):
        return z_at[dz] * WIDE + x_at[dx]

    peers = [(chip_at(dz, dx) * 2 + core, y) for dz, dx in FAR_FIRST]
    peers += [(dp, ring(k)) for k in (2, 1, 3)] + [sibling]
    for device in peers:
        pl.semaphore_signal(barrier, inc=1, device_id=device, device_id_type=MESH)
    for k in order:
        load_tok[k].start()
    load_ups.start()
    for k in (2, 3, 1, 0):
        load_w[k].start()

    tag = jnp.full((TILE, LANE), adapter[0, 0], jnp.int32).astype(F32)
    for copy in load_items:
        copy.wait()
    for t in range(CHIPS):
        down_rows = (t % 4) * TILE
        lanes = (t // 4) * LANE
        if t % 2 == 0:
            pair = item[down_rows:down_rows + 2 * TILE, lanes:lanes + LANE].astype(F32)
        half = pair[(t % 2) * TILE:(t % 2 + 1) * TILE]
        s1[t] = jnp.concatenate([half, tag], axis=0).astype(BF16)
    for k in order:
        load_tok[k].wait()

    pl.semaphore_wait(barrier, len(peers))

    up_dev, dn_dev = (dp, ring(1)), (dp, ring(3))

    def spread(phase, src, dst, mine):
        for dz, dx in FAR_FIRST:
            to = chip_at(dz, dx)
            pltpu.make_async_remote_copy(
                src_ref=src.at[to], dst_ref=dst(chip), send_sem=ph_s.at[phase],
                recv_sem=ph_r.at[phase], device_id=(to * 2 + core, y), device_id_type=MESH,
            ).start()
        pltpu.make_async_copy(src.at[chip], dst(chip), ph_r.at[phase]).start()
        return pltpu.make_async_copy(mine, mine, ph_r.at[phase])

    def drain(phase, src):
        others = src.at[pl.ds(0, CHIPS - 1)]
        pltpu.make_async_copy(others, others, ph_s.at[phase]).wait()

    def arrive(copies):
        for copy in copies:
            copy.wait_recv()

    def token_send(c, owner_y, index, device):
        return push(tok.at[c, here(owner_y)], tok.at[c, here(owner_y)], ag_s.at[index], ag_r.at[index], device)

    first = spread(0, s1, lambda i: r1.at[core, i], r1.at[core])
    ag_up = [token_send(ring(2), y, 0, up_dev)]
    ag_dn = [token_send(ring(3), y, 6, dn_dev)]
    ag_up.append(token_send(ring(1), y, 1, up_dev))
    ag_dn.append(token_send(ring(0), y, 7, dn_dev))
    ag_up.append(token_send(ring(3), y, 2, up_dev))
    ag_dn.append(token_send(ring(2), y, 8, dn_dev))
    ag_up.append(token_send(ring(0), y, 3, up_dev))
    ag_dn.append(token_send(ring(1), y, 9, dn_dev))

    def backward(k):
        c = ring(k)
        load_w[k].wait()
        if k == 2:
            load_ups.wait()
        part[c] = dot_t(ups[...], w[c])
        if k:
            send[c] = part[c].astype(BF16)

    adapters = owner.shape[1]
    out_rows, tagged_rows = CHIPS * TILE, CHIPS * TAGGED
    pick = one_hot(
        ids(out_rows, tagged_rows, 1) == ((ids(out_rows, tagged_rows, 0) >> 3) << 4) + TILE
    )

    def users(got):
        tags = dot(pick, got).astype(jnp.int32)[:, 0:adapters]
        return one_hot(tags == ids(out_rows, adapters, 1))

    def owners(n_rows, shift, which):
        return one_hot(owner[...] == (ids(n_rows, adapters, 0) >> shift) * 2 + which)

    slots_a = owners(tagged_rows, 4, core)
    slots_b = owners(tagged_rows, 4, other)
    same = (ids(out_rows, tagged_rows, 0) & 7) == (ids(out_rows, tagged_rows, 1) & 15)
    same_back = (ids(out_rows, out_rows, 0) & 7) == (ids(out_rows, out_rows, 1) & 7)

    backward(2)
    backward(3)
    ag_up[0].wait_recv()
    ag_up.append(token_send(ring(1), ring(3), 4, up_dev))
    ag_dn[0].wait_recv()
    ag_dn.append(token_send(ring(0), ring(1), 10, dn_dev))

    first.wait()
    swap = push(r1.at[core], r1.at[core], ph_s.at[1], ph_r.at[1], sibling)
    got = r1[core].reshape(tagged_rows, LANE)
    users_a = users(got)
    take_a = jnp.where(same, dot_t(users_a, slots_a), 0.0).astype(BF16)
    take_b = jnp.where(same, dot_t(users_a, slots_b), 0.0).astype(BF16)
    chosen = dot(take_a, got)
    swap.wait_recv()
    got = r1[other].reshape(tagged_rows, LANE)
    s3[...] = (chosen + dot(take_b, got)).reshape(CHIPS, TILE, LANE)
    second = spread(2, s3, lambda i: r3.at[i], r3)

    ag_up[1].wait_recv()
    ag_up.append(token_send(ring(0), ring(3), 5, up_dev))
    ag_dn[1].wait_recv()
    ag_dn.append(token_send(ring(1), ring(1), 11, dn_dev))

    slots_back = owners(out_rows, 3, core)
    back_a[...] = jnp.where(same_back, dot_t(slots_back, users_a), 0.0).astype(BF16)
    back_b[...] = jnp.where(same_back, dot_t(slots_back, users(got)), 0.0).astype(BF16)

    backward(1)

    def rows_send(c, to, dst, index, device):
        return push(send.at[c, here(to)], dst, rs_s.at[index], rs_r.at[index], device)

    far_up = [
        rows_send(ring(2), ring(2), relay_up.at[0], 0, up_dev),
        rows_send(ring(3), ring(2), relay_up.at[1], 1, up_dev),
    ]
    far_dn = [rows_send(ring(1), ring(2), relay_dn.at[0], 6, dn_dev)]
    near_up = [rows_send(ring(3), ring(1), got_up.at[ring(3)], 2, up_dev)]
    near_dn = [rows_send(ring(3), ring(3), got_dn.at[ring(3)], 8, dn_dev)]

    backward(0)
    ag_up[4].wait_recv()
    mix[...] = dot(tok[y], w[y])

    second.wait()

    def half_item(base):
        return jnp.concatenate(
            [
                jnp.concatenate([r3[lane * 4 + base], r3[lane * 4 + base + 1]], axis=0)
                for lane in range(cols // LANE)
            ],
            axis=1,
        ).astype(BF16)

    down_here, up_here = half_item(0), half_item(2)
    low_all[y, RANK:, :] = dot_t(up_here, ups[...])
    low_all[y, 0:RANK, :] = dot_t(down_here, tok[y])
    lows = [
        push(low_all.at[y], low_all.at[y], low_s.at[k - 1], low_r.at[k - 1], (dp, ring(k)))
        for k in (2, 1, 3)
    ]

    def relayed(c, to, relay, dst, index, device):
        send[c, here(to), :] = (part[c, here(to), :] + relay[...].astype(F32)).astype(BF16)
        return rows_send(c, to, dst, index, device)

    far_up[0].wait_recv()
    near_up.append(relayed(ring(1), ring(1), relay_up.at[0], got_up.at[ring(1)], 3, up_dev))
    far_dn[0].wait_recv()
    near_dn.append(relayed(ring(2), ring(3), relay_dn.at[0], got_dn.at[ring(2)], 9, dn_dev))
    far_up[1].wait_recv()
    near_up.append(relayed(ring(2), ring(1), relay_up.at[1], got_up.at[ring(2)], 4, up_dev))

    ag_up[2].wait_recv()
    ag_up[3].wait_recv()
    ag_up[5].wait_recv()
    ag_dn[2].wait_recv()
    ag_dn[3].wait_recv()
    ag_dn[4].wait_recv()
    ag_dn[5].wait_recv()
    mix[...] += dot(tok[ring(1)], w[ring(1)])

    arrive(lows)
    total = low_all[0] + low_all[1] + low_all[2] + low_all[3]
    low_t = total[0:RANK].astype(BF16)
    back_t = total[RANK:].astype(BF16)

    down_term = 2.0 * dot(back_t, tok[y])
    up_term = 2.0 * dot(low_t, ups[...])
    for t in range(CHIPS):
        source = down_term if t % 4 < 2 else up_term
        lanes = (t // 4) * LANE
        g1[t] = source[(t % 2) * TILE:(t % 2 + 1) * TILE, lanes:lanes + LANE]
    first = spread(3, g1, lambda i: h1.at[core, i], h1.at[core])

    flat = total.T
    low = flat[:, 0:RANK].astype(BF16)
    back = flat[:, RANK:].astype(BF16)
    part[y] = part[y] + 2.0 * dot(back, down_here)
    send[y] = part[y].astype(BF16)
    far_dn.append(rows_send(y, ring(2), relay_dn.at[1], 7, dn_dev))
    near_up.append(rows_send(y, ring(1), got_up.at[y], 5, up_dev))
    near_dn.append(rows_send(y, ring(3), got_dn.at[y], 10, dn_dev))
    mix[...] += 2.0 * dot(low, up_here) + dot(tok[ring(3)], w[ring(3)])

    first.wait()
    swap = push(h1.at[core], h1.at[core], ph_s.at[4], ph_r.at[4], sibling)
    owned = dot(back_a[...], h1[core].reshape(out_rows, LANE).astype(BF16))
    swap.wait_recv()
    owned += dot(back_b[...], h1[other].reshape(out_rows, LANE).astype(BF16))
    g3[...] = owned.reshape(CHIPS, TILE, LANE)
    second = spread(5, g3, lambda i: h3.at[i], h3)

    far_dn[1].wait_recv()
    near_dn.append(relayed(ring(1), ring(3), relay_dn.at[1], got_dn.at[ring(1)], 11, dn_dev))
    mixed_out[...] = (mix[...] + dot(tok[ring(2)], w[ring(2)])).astype(BF16)

    drain(0, s1)
    drain(2, s3)
    drain(3, g1)
    arrive(near_up)
    arrive(near_dn)
    for c in range(RING):
        grad_out[:, c * cols:(c + 1) * cols] = (
            part[c, here(y), :] + got_up[c].astype(F32) + got_dn[c].astype(F32)
        ).astype(BF16)
    for copy in sent:
        copy.wait_send()

    second.wait()
    for t in range(CHIPS):
        target = down_out if t % 4 < 2 else up_out
        lanes = (t // 4) * LANE
        target[0, (t % 2) * TILE:(t % 2 + 1) * TILE, lanes:lanes + LANE] = h3[t]
    drain(5, g3)


def per_device(tokens, weight, down, up, upstream, adapter, owner):
    rows, width = tokens.shape
    block, cols = upstream.shape
    any_spec = pl.BlockSpec(memory_space=pl.ANY)
    dma = lambda *shape: pltpu.SemaphoreType.DMA(shape)
    tiles = lambda *lead: pltpu.VMEM((*lead, CHIPS, TILE, LANE), F32)
    scratch = [
        pltpu.VMEM((RING, cols, cols), BF16),
        pltpu.VMEM((RING, block, cols), BF16),
        pltpu.VMEM((block, cols), BF16),
        pltpu.VMEM((RING, block, cols), F32),
        pltpu.VMEM((RING, block, cols), BF16),
        pltpu.VMEM((2, rows, cols), BF16),
        pltpu.VMEM((2, rows, cols), BF16),
        pltpu.VMEM((RING, rows, cols), BF16),
        pltpu.VMEM((RING, rows, cols), BF16),
        pltpu.VMEM((block, cols), F32),
        pltpu.VMEM((ITEM, cols), BF16),
        pltpu.VMEM((CHIPS, TAGGED, LANE), BF16),
        pltpu.VMEM((2, CHIPS, TAGGED, LANE), BF16),
        tiles(), tiles(), tiles(), tiles(2), tiles(), tiles(),
        pltpu.VMEM((RING, ITEM, block), F32),
        pltpu.VMEM((CHIPS * TILE, CHIPS * TILE), BF16),
        pltpu.VMEM((CHIPS * TILE, CHIPS * TILE), BF16),
        dma(11), dma(12), dma(12), dma(12), dma(12), dma(3), dma(3), dma(6), dma(6),
    ]
    return pl.pallas_call(
        kernel,
        out_shape=(
            pltpu.VMEM((block, cols), BF16),
            pltpu.VMEM((rows, width), BF16),
            pltpu.VMEM(down.shape, F32),
            pltpu.VMEM(up.shape, F32),
        ),
        in_specs=[any_spec] * 5
        + [pl.BlockSpec(memory_space=pltpu.SMEM), pl.BlockSpec(memory_space=pltpu.VMEM)],
        out_specs=(pl.BlockSpec(memory_space=pltpu.VMEM),) * 4,
        scratch_shapes=scratch,
        compiler_params=pltpu.CompilerParams(
            collective_id=0, has_side_effects=True, vmem_limit_bytes=63000 * 1024
        ),
        cost_estimate=pl.CostEstimate(
            flops=4 * block * width * cols, bytes_accessed=12 * 1024 * 1024, transcendentals=0
        ),
    )(tokens, weight, down, up, upstream, adapter, owner.reshape(1, -1))


def solution(mesh):
    return jax.shard_map(
        per_device,
        mesh=mesh,
        in_specs=(
            P(("dp", "tensor"), None),
            P(None, "tensor"),
            P("dp", None, "tensor"),
            P("dp", None, "tensor"),
            P("dp", "tensor"),
            P("dp", None),
            P(),
        ),
        out_specs=(
            P("dp", "tensor"),
            P(("dp", "tensor"), None),
            P("dp", None, "tensor"),
            P("dp", None, "tensor"),
        ),
        check_vma=False,
    )
```

```python
import jax
import jax.numpy as jnp
from jax import lax
from jax.experimental import pallas as pl
from jax.experimental.pallas import tpu as pltpu
from jax.sharding import PartitionSpec as P

MESH = pl.DeviceIdType.MESH
DEEP = 8
WIDE = 4
CHIPS = DEEP * WIDE
RING = 4
RANK = 16
ITEM = 2 * RANK
LANE = 128
MIDS = 16
HALF = MIDS // 2
PIECES = [(dz, dx) for dz in (0, 2, 1, 3) for dx in (2, 1, 3, 0)]
FAR_FIRST = [
    (dz, dx) for dz in (4, 3, 5, 2, 6, 1, 7, 0) for dx in (2, 1, 3, 0) if dz or dx
]

F32 = jnp.float32
BF16 = jnp.bfloat16


def dot(a, b):
    return jnp.dot(a, b, preferred_element_type=F32)


def dot_t(a, b):
    return lax.dot_general(a, b, (((1,), (1,)), ((), ())), preferred_element_type=F32)


def one_hot(condition):
    return condition.astype(F32).astype(BF16)


def ids(rows, cols, dim):
    return lax.broadcasted_iota(jnp.int32, (rows, cols), dim)


def kernel(
    tokens, weight, down, up, upstream, adapter, owner,
    mixed_out, grad_out, down_out, up_out,
    w, tok, ups, part, send, relay_up, relay_dn, got_up, got_dn, mix,
    item, tag, tags, r1, s3, r3, g1, h1, g3, h3, low_all, back_a, back_b, block_id, owner_row,
    local_sem, ag_s, ag_r, rs_s, rs_r, low_s, low_r, ph_s, ph_r, ready,
):
    dp = lax.axis_index("dp")
    y = lax.axis_index("tensor")
    chip, core = dp // 2, dp % 2
    other = 1 - core
    is_mid = chip < MIDS
    z, x = chip // WIDE, chip % WIDE
    z_at = [lax.rem(z + j, DEEP) for j in range(DEEP)]
    x_at = [lax.rem(x + j, WIDE) for j in range(WIDE)]
    rows = tokens.shape[0]
    cols = weight.shape[1]
    ring_at = [lax.rem(y + j, RING) for j in range(RING)]
    sibling = (chip * 2 + other, y)

    def ring(step):
        return ring_at[step]

    def here(c):
        return pl.ds(pl.multiple_of(c * rows, rows), rows)

    def wide(c):
        return pl.ds(pl.multiple_of(c * cols, cols), cols)

    sent = []

    def push(src, dst, ssem, rsem, device):
        copy = pltpu.make_async_remote_copy(
            src_ref=src, dst_ref=dst, send_sem=ssem, recv_sem=rsem,
            device_id=device, device_id_type=MESH,
        )
        copy.start()
        sent.append(copy)
        return copy

    load_items = [
        pltpu.make_async_copy(down.at[0], item.at[pl.ds(0, RANK)], local_sem.at[0]),
        pltpu.make_async_copy(up.at[0], item.at[pl.ds(RANK, RANK)], local_sem.at[1]),
    ]
    order = (2, 1, 3, 0)
    load_tok = [
        pltpu.make_async_copy(
            tokens.at[:, wide(ring(k))], tok.at[ring(k), here(y)], local_sem.at[2 + k]
        )
        for k in range(RING)
    ]
    load_ups = pltpu.make_async_copy(upstream, ups, local_sem.at[6])
    load_w = [
        pltpu.make_async_copy(weight.at[wide(ring(k))], w.at[ring(k)], local_sem.at[7 + k])
        for k in range(RING)
    ]
    load_ids = [
        pltpu.make_async_copy(adapter, block_id, local_sem.at[11]),
        pltpu.make_async_copy(owner, owner_row, local_sem.at[12]),
    ]

    barrier = pltpu.get_barrier_semaphore()

    def chip_at(dz, dx):
        return z_at[dz] * WIDE + x_at[dx]

    @pl.when(is_mid)
    def _():
        for dz, dx in FAR_FIRST:
            device = (chip_at(dz, dx) * 2 + core, y)
            pl.semaphore_signal(barrier, inc=1, device_id=device, device_id_type=MESH)

    for device in [(dp, ring(k)) for k in (2, 1, 3)] + [sibling]:
        pl.semaphore_signal(barrier, inc=1, device_id=device, device_id_type=MESH)
    for copy in load_items + load_ids:
        copy.start()
    for k in order:
        load_tok[k].start()
    load_ups.start()
    for k in (2, 3, 1, 0):
        load_w[k].start()
    for copy in load_items + load_ids:
        copy.wait()
    tag[...] = jnp.broadcast_to(block_id[...].astype(F32), (1, LANE))
    for k in order:
        load_tok[k].wait()

    pl.semaphore_wait(barrier, jnp.where(is_mid, MIDS - 1, MIDS) + RING)

    up_dev, dn_dev = (dp, ring(1)), (dp, ring(3))

    def push_to(src, dst, phase, device):
        pltpu.make_async_remote_copy(
            src_ref=src, dst_ref=dst, send_sem=ph_s.at[phase], recv_sem=ph_r.at[phase],
            device_id=device, device_id_type=MESH,
        ).start()

    def piece(src, u):
        return src.at[
            pl.ds(pl.multiple_of(u // HALF * RANK, RANK), RANK),
            pl.ds(pl.multiple_of(u % HALF * LANE, LANE), LANE),
        ]

    def gather(phase, src, dst):
        for dz, dx in PIECES:
            u = lax.rem(z + dz, MIDS // WIDE) * WIDE + x_at[dx]
            if dz or dx:
                push_to(piece(src, u), dst.at[core, chip], phase, (u * 2 + core, y))
            else:
                @pl.when(is_mid)
                def _():
                    pltpu.make_async_copy(piece(src, u), dst.at[core, chip], ph_r.at[phase]).start()

                @pl.when(jnp.logical_not(is_mid))
                def _():
                    push_to(piece(src, u), dst.at[core, chip], phase, (u * 2 + core, y))

    def drain_gather(phase, like):
        @pl.when(is_mid)
        def _():
            part_of = like.at[pl.ds(0, MIDS - 1)]
            pltpu.make_async_copy(part_of, part_of, ph_s.at[phase]).wait()

        @pl.when(jnp.logical_not(is_mid))
        def _():
            part_of = like.at[pl.ds(0, MIDS)]
            pltpu.make_async_copy(part_of, part_of, ph_s.at[phase]).wait()

    def spread(phase, src, dst):
        for dz, dx in FAR_FIRST:
            to = chip_at(dz, dx)
            push_to(src.at[to], dst.at[chip], phase, (to * 2 + core, y))
        pltpu.make_async_copy(src.at[chip], dst.at[chip], ph_r.at[phase]).start()

    def drain_spread(phase, src):
        others = src.at[pl.ds(0, CHIPS - 1)]
        pltpu.make_async_copy(others, others, ph_s.at[phase]).wait()

    def landed(phase, dst):
        pltpu.make_async_copy(dst, dst, ph_r.at[phase]).wait()

    def swap(phase, both):
        copy = pltpu.make_async_remote_copy(
            src_ref=both.at[core], dst_ref=both.at[core], send_sem=ph_s.at[phase],
            recv_sem=ph_r.at[phase], device_id=sibling, device_id_type=MESH,
        )
        copy.start()
        return copy

    def arrive(copies):
        for copy in copies:
            copy.wait_recv()

    def token_send(c, owner_y, index, device):
        return push(tok.at[c, here(owner_y)], tok.at[c, here(owner_y)], ag_s.at[index], ag_r.at[index], device)

    gather(0, item, r1)
    for dz, dx in PIECES:
        u = lax.rem(z + dz, MIDS // WIDE) * WIDE + x_at[dx]
        if dz or dx:
            push_to(tag, tags.at[core, chip], 1, (u * 2 + core, y))
        else:
            @pl.when(is_mid)
            def _():
                pltpu.make_async_copy(tag, tags.at[core, chip], ph_r.at[1]).start()

            @pl.when(jnp.logical_not(is_mid))
            def _():
                push_to(tag, tags.at[core, chip], 1, (u * 2 + core, y))
    ag_up = [token_send(ring(2), y, 0, up_dev)]
    ag_dn = [token_send(ring(3), y, 6, dn_dev)]
    ag_up.append(token_send(ring(1), y, 1, up_dev))
    ag_dn.append(token_send(ring(0), y, 7, dn_dev))
    ag_up.append(token_send(ring(3), y, 2, up_dev))
    ag_dn.append(token_send(ring(2), y, 8, dn_dev))
    ag_up.append(token_send(ring(0), y, 3, up_dev))
    ag_dn.append(token_send(ring(1), y, 9, dn_dev))

    def backward(k):
        c = ring(k)
        load_w[k].wait()
        if k == 2:
            load_ups.wait()
        part[c] = dot_t(ups[...], w[c])
        if k:
            send[c] = part[c].astype(BF16)

    @pl.when(jnp.logical_not(is_mid))
    def _():
        for u in range(MIDS):
            pl.semaphore_signal(ready, inc=1, device_id=(u * 2 + core, y), device_id_type=MESH)

    adapters = owner_row.shape[1]
    span = CHIPS * RANK
    same = (ids(span, span, 0) & (RANK - 1)) == (ids(span, span, 1) & (RANK - 1))

    def users(which):
        found = jnp.broadcast_to(tags[which], (CHIPS, RANK, LANE)).reshape(span, LANE)
        return one_hot(found[:, 0:adapters].astype(jnp.int32) == ids(span, adapters, 1))

    def owners(which):
        return one_hot(owner_row[...] == (ids(span, adapters, 0) >> 4) * 2 + which)

    def matched(a, b):
        return jnp.where(same, dot_t(a, b), 0.0).astype(BF16)

    def flat(pieces):
        return pieces.reshape(span, LANE)

    backward(2)
    backward(3)

    @pl.when(is_mid)
    def _():
        landed(0, r1.at[core])
        trade = swap(2, r1)
        landed(1, tags.at[core])
        trade_tags = swap(3, tags)
        asks = users(core)
        chosen = dot(matched(asks, owners(core)), flat(r1[core]))
        take_b = matched(asks, owners(other))
        pl.semaphore_wait(ready, CHIPS - MIDS)
        trade.wait_recv()
        s3[...] = (chosen + dot(take_b, flat(r1[other]))).astype(BF16).reshape(CHIPS, RANK, LANE)
        spread(4, s3, r3)
        slots = owners(core)
        back_a[...] = matched(slots, users(core))
        trade_tags.wait_recv()
        back_b[...] = matched(slots, users(other))
        trade.wait_send()
        trade_tags.wait_send()

    ag_up[0].wait_recv()
    ag_up.append(token_send(ring(1), ring(3), 4, up_dev))
    ag_dn[0].wait_recv()
    ag_dn.append(token_send(ring(0), ring(1), 10, dn_dev))
    ag_up[1].wait_recv()
    ag_up.append(token_send(ring(0), ring(3), 5, up_dev))
    ag_dn[1].wait_recv()
    ag_dn.append(token_send(ring(1), ring(1), 11, dn_dev))

    backward(1)

    def rows_send(c, to, dst, index, device):
        return push(send.at[c, here(to)], dst, rs_s.at[index], rs_r.at[index], device)

    far_up = [
        rows_send(ring(2), ring(2), relay_up.at[0], 0, up_dev),
        rows_send(ring(3), ring(2), relay_up.at[1], 1, up_dev),
    ]
    far_dn = [rows_send(ring(1), ring(2), relay_dn.at[0], 6, dn_dev)]
    near_up = [rows_send(ring(3), ring(1), got_up.at[ring(3)], 2, up_dev)]
    near_dn = [rows_send(ring(3), ring(3), got_dn.at[ring(3)], 8, dn_dev)]

    backward(0)
    ag_up[4].wait_recv()
    mix[...] = dot(tok[y], w[y])

    landed(4, r3)
    down_here = jnp.concatenate([r3[u] for u in range(HALF)], axis=1)
    up_here = jnp.concatenate([r3[HALF + u] for u in range(HALF)], axis=1)
    low_all[y, RANK:, :] = dot_t(up_here, ups[...])
    low_all[y, 0:RANK, :] = dot_t(down_here, tok[y])
    lows = [
        push(low_all.at[y], low_all.at[y], low_s.at[k - 1], low_r.at[k - 1], (dp, ring(k)))
        for k in (2, 1, 3)
    ]

    def relayed(c, to, relay, dst, index, device):
        send[c, here(to), :] = (part[c, here(to), :] + relay[...].astype(F32)).astype(BF16)
        return rows_send(c, to, dst, index, device)

    far_up[0].wait_recv()
    near_up.append(relayed(ring(1), ring(1), relay_up.at[0], got_up.at[ring(1)], 3, up_dev))
    far_dn[0].wait_recv()
    near_dn.append(relayed(ring(2), ring(3), relay_dn.at[0], got_dn.at[ring(2)], 9, dn_dev))
    far_up[1].wait_recv()
    near_up.append(relayed(ring(2), ring(1), relay_up.at[1], got_up.at[ring(2)], 4, up_dev))

    ag_up[2].wait_recv()
    ag_up[3].wait_recv()
    ag_up[5].wait_recv()
    ag_dn[2].wait_recv()
    ag_dn[3].wait_recv()
    ag_dn[4].wait_recv()
    ag_dn[5].wait_recv()
    mix[...] += dot(tok[ring(1)], w[ring(1)])

    arrive(lows)
    total = low_all[0] + low_all[1] + low_all[2] + low_all[3]
    low_t = total[0:RANK].astype(BF16)
    back_t = total[RANK:].astype(BF16)

    g1[0:RANK, :] = (2.0 * dot(back_t, tok[y])).astype(BF16)
    g1[RANK:, :] = (2.0 * dot(low_t, ups[...])).astype(BF16)
    gather(5, g1, h1)

    turned = total.T
    low = turned[:, 0:RANK].astype(BF16)
    back = turned[:, RANK:].astype(BF16)
    part[y] = part[y] + 2.0 * dot(back, down_here)
    send[y] = part[y].astype(BF16)
    far_dn.append(rows_send(y, ring(2), relay_dn.at[1], 7, dn_dev))
    near_up.append(rows_send(y, ring(1), got_up.at[y], 5, up_dev))
    near_dn.append(rows_send(y, ring(3), got_dn.at[y], 10, dn_dev))
    mix[...] += 2.0 * dot(low, up_here) + dot(tok[ring(3)], w[ring(3)])

    @pl.when(is_mid)
    def _():
        landed(5, h1.at[core])
        trade = swap(6, h1)
        owned = dot(back_a[...], flat(h1[core]))
        trade.wait_recv()
        owned += dot(back_b[...], flat(h1[other]))
        g3[...] = owned.astype(BF16).reshape(CHIPS, RANK, LANE)
        spread(7, g3, h3)
        trade.wait_send()

    far_dn[1].wait_recv()
    near_dn.append(relayed(ring(1), ring(3), relay_dn.at[1], got_dn.at[ring(1)], 11, dn_dev))
    mixed_out[...] = (mix[...] + dot(tok[ring(2)], w[ring(2)])).astype(BF16)

    drain_gather(0, r3)
    drain_gather(1, tags.at[core])
    drain_gather(5, r3)
    arrive(near_up)
    arrive(near_dn)
    for c in range(RING):
        grad_out[:, c * cols:(c + 1) * cols] = (
            part[c, here(y), :] + got_up[c].astype(F32) + got_dn[c].astype(F32)
        ).astype(BF16)
    for copy in sent:
        copy.wait_send()

    landed(7, h3)
    for u in range(HALF):
        lanes = slice(u * LANE, (u + 1) * LANE)
        down_out[0, :, lanes] = h3[u].astype(F32)
        up_out[0, :, lanes] = h3[HALF + u].astype(F32)

    @pl.when(is_mid)
    def _():
        drain_spread(4, s3)
        drain_spread(7, g3)


def per_device(tokens, weight, down, up, upstream, adapter, owner):
    rows, width = tokens.shape
    block, cols = upstream.shape
    any_spec = pl.BlockSpec(memory_space=pl.ANY)
    dma = lambda *shape: pltpu.SemaphoreType.DMA(shape)
    pieces = lambda *lead: pltpu.VMEM((*lead, RANK, LANE), BF16)
    scratch = [
        pltpu.VMEM((RING, cols, cols), BF16),
        pltpu.VMEM((RING, block, cols), BF16),
        pltpu.VMEM((block, cols), BF16),
        pltpu.VMEM((RING, block, cols), F32),
        pltpu.VMEM((RING, block, cols), BF16),
        pltpu.VMEM((2, rows, cols), BF16),
        pltpu.VMEM((2, rows, cols), BF16),
        pltpu.VMEM((RING, rows, cols), BF16),
        pltpu.VMEM((RING, rows, cols), BF16),
        pltpu.VMEM((block, cols), F32),
        pltpu.VMEM((ITEM, cols), BF16),
        pltpu.VMEM((1, LANE), F32),
        pltpu.VMEM((2, CHIPS, 1, LANE), F32),
        pieces(2, CHIPS), pieces(CHIPS), pieces(MIDS),
        pltpu.VMEM((ITEM, cols), BF16),
        pieces(2, CHIPS), pieces(CHIPS), pieces(MIDS),
        pltpu.VMEM((RING, ITEM, block), F32),
        pltpu.VMEM((CHIPS * RANK, CHIPS * RANK), BF16),
        pltpu.VMEM((CHIPS * RANK, CHIPS * RANK), BF16),
        pltpu.VMEM(adapter.shape, jnp.int32),
        pltpu.VMEM((1, owner.shape[0]), jnp.int32),
        dma(13), dma(12), dma(12), dma(12), dma(12), dma(3), dma(3), dma(8), dma(8),
        pltpu.SemaphoreType.REGULAR,
    ]
    return pl.pallas_call(
        kernel,
        out_shape=(
            pltpu.VMEM((block, cols), BF16),
            pltpu.VMEM((rows, width), BF16),
            pltpu.VMEM(down.shape, F32),
            pltpu.VMEM(up.shape, F32),
        ),
        in_specs=[any_spec] * 5 + [pl.BlockSpec(memory_space=pltpu.HBM), any_spec],
        out_specs=(pl.BlockSpec(memory_space=pltpu.VMEM),) * 4,
        scratch_shapes=scratch,
        compiler_params=pltpu.CompilerParams(
            collective_id=0, has_side_effects=True, vmem_limit_bytes=63000 * 1024
        ),
        cost_estimate=pl.CostEstimate(
            flops=4 * block * width * cols, bytes_accessed=12 * 1024 * 1024, transcendentals=0
        ),
    )(tokens, weight, down, up, upstream, adapter, owner.reshape(1, -1))


def solution(mesh):
    return jax.shard_map(
        per_device,
        mesh=mesh,
        in_specs=(
            P(("dp", "tensor"), None),
            P(None, "tensor"),
            P("dp", None, "tensor"),
            P("dp", None, "tensor"),
            P("dp", "tensor"),
            P("dp", None),
            P(),
        ),
        out_specs=(
            P("dp", "tensor"),
            P(("dp", "tensor"), None),
            P("dp", None, "tensor"),
            P("dp", None, "tensor"),
        ),
        check_vma=False,
    )
```

```python
import jax
import jax.numpy as jnp
from jax import lax
from jax.experimental import pallas as pl
from jax.experimental.pallas import tpu as pltpu
from jax.sharding import PartitionSpec as P

MESH = pl.DeviceIdType.MESH
DEEP = 8
WIDE = 4
CHIPS = DEEP * WIDE
RING = 4
RANK = 16
ITEM = 2 * RANK
LANE = 128
CORES = 2 * CHIPS
MIDS = CORES // 2
EIGHT = 8
SPAN = CORES * EIGHT
PIECES = [(dz, dx, dc) for dz in (4, 6, 2, 0) for dx in (2, 1, 3, 0) for dc in (0, 1)]
EVERY = [
    (dz, dx, dc) for dz in (4, 3, 5, 2, 6, 1, 7, 0) for dx in (2, 1, 3, 0) for dc in (0, 1)
]

F32 = jnp.float32
BF16 = jnp.bfloat16


def dot(a, b):
    return jnp.dot(a, b, preferred_element_type=F32)


def dot_t(a, b):
    return lax.dot_general(a, b, (((1,), (1,)), ((), ())), preferred_element_type=F32)


def one_hot(condition):
    return condition.astype(F32).astype(BF16)


def ids(rows, cols, dim):
    return lax.broadcasted_iota(jnp.int32, (rows, cols), dim)


def kernel(
    tokens, weight, down, up, upstream, adapter, owner,
    mixed_out, grad_out, down_out, up_out,
    w, tok, ups, part, send, relay_up, relay_dn, got_up, got_dn, mix,
    item, tag, tags, s1, r1, s3, r3, g1, h1, g3, h3, low_all, back, block_id, owner_row,
    local_sem, ag_s, ag_r, rs_s, rs_r, low_s, low_r, ph_s, ph_r, ready,
):
    dp = lax.axis_index("dp")
    y = lax.axis_index("tensor")
    chip, core = dp // 2, dp % 2
    z, x = chip // WIDE, chip % WIDE
    is_mid = z % 2 == 0
    mine = z // 2 * (2 * WIDE) + x * 2 + core
    z_at = [lax.rem(z + j, DEEP) for j in range(DEEP)]
    x_at = [lax.rem(x + j, WIDE) for j in range(WIDE)]
    rows = tokens.shape[0]
    cols = weight.shape[1]
    ring_at = [lax.rem(y + j, RING) for j in range(RING)]
    z_mid = [lax.rem(z // 2 + j, DEEP // 2) for j in range(DEEP // 2)]
    cores = [core, 1 - core]

    def ring(step):
        return ring_at[step]

    def here(c):
        return pl.ds(pl.multiple_of(c * rows, rows), rows)

    def wide(c):
        return pl.ds(pl.multiple_of(c * cols, cols), cols)

    sent = []

    def push(src, dst, ssem, rsem, device):
        copy = pltpu.make_async_remote_copy(
            src_ref=src, dst_ref=dst, send_sem=ssem, recv_sem=rsem,
            device_id=device, device_id_type=MESH,
        )
        copy.start()
        sent.append(copy)
        return copy

    load_items = [
        pltpu.make_async_copy(down.at[0], item.at[pl.ds(0, RANK)], local_sem.at[0]),
        pltpu.make_async_copy(up.at[0], item.at[pl.ds(RANK, RANK)], local_sem.at[1]),
    ]
    order = (2, 1, 3, 0)
    load_tok = [
        pltpu.make_async_copy(
            tokens.at[:, wide(ring(k))], tok.at[ring(k), here(y)], local_sem.at[2 + k]
        )
        for k in range(RING)
    ]
    load_ups = pltpu.make_async_copy(upstream, ups, local_sem.at[6])
    load_w = [
        pltpu.make_async_copy(weight.at[wide(ring(k))], w.at[ring(k)], local_sem.at[7 + k])
        for k in range(RING)
    ]
    load_ids = [
        pltpu.make_async_copy(adapter, block_id, local_sem.at[11]),
        pltpu.make_async_copy(owner, owner_row, local_sem.at[12]),
    ]

    barrier = pltpu.get_barrier_semaphore()

    def at(dz, dx, dc):
        return z_at[dz] * (2 * WIDE) + x_at[dx] * 2 + cores[dc]

    @pl.when(is_mid)
    def _():
        for step in EVERY:
            if any(step):
                pl.semaphore_signal(barrier, inc=1, device_id=(at(*step), y), device_id_type=MESH)

    for k in (2, 1, 3):
        pl.semaphore_signal(barrier, inc=1, device_id=(dp, ring(k)), device_id_type=MESH)
    for copy in load_items + load_ids:
        copy.start()
    for k in order:
        load_tok[k].start()
    load_ups.start()
    for k in (2, 3, 1, 0):
        load_w[k].start()
    for copy in load_items + load_ids:
        copy.wait()
    tag[...] = jnp.broadcast_to(block_id[...].astype(F32), (1, LANE))
    for v in range(MIDS):
        lanes = (v // 4) * LANE
        if v % 2 == 0:
            pair = item[v % 4 * EIGHT:v % 4 * EIGHT + RANK, lanes:lanes + LANE].astype(F32)
        s1[v] = pair[(v % 2) * EIGHT:(v % 2 + 1) * EIGHT].astype(BF16)
    for k in order:
        load_tok[k].wait()

    pl.semaphore_wait(barrier, jnp.where(is_mid, MIDS - 1, MIDS) + RING - 1)

    up_dev, dn_dev = (dp, ring(1)), (dp, ring(3))

    def push_to(src, dst, phase, device):
        pltpu.make_async_remote_copy(
            src_ref=src, dst_ref=dst, send_sem=ph_s.at[phase], recv_sem=ph_r.at[phase],
            device_id=device, device_id_type=MESH,
        ).start()

    def gather(pairs):
        for dz, dx, dc in PIECES:
            mid = z_mid[dz // 2] * (2 * WIDE) + x_at[dx] * 2 + cores[dc]
            to = z_mid[dz // 2] * (4 * WIDE) + x_at[dx] * 2 + cores[dc]

            def move():
                for phase, src, dst in pairs:
                    push_to(src(mid), dst.at[dp], phase, (to, y))

            if dz or dx or dc:
                move()
            else:
                @pl.when(is_mid)
                def _():
                    for phase, src, dst in pairs:
                        pltpu.make_async_copy(src(mid), dst.at[dp], ph_r.at[phase]).start()

                pl.when(jnp.logical_not(is_mid))(move)

    def drain_gather(phase, like):
        @pl.when(is_mid)
        def _():
            part_of = like.at[pl.ds(0, MIDS - 1)]
            pltpu.make_async_copy(part_of, part_of, ph_s.at[phase]).wait()

        @pl.when(jnp.logical_not(is_mid))
        def _():
            part_of = like.at[pl.ds(0, MIDS)]
            pltpu.make_async_copy(part_of, part_of, ph_s.at[phase]).wait()

    def spread(phase, src, dst):
        for step in EVERY:
            to = at(*step)
            if any(step):
                push_to(src.at[to], dst.at[mine], phase, (to, y))
            else:
                pltpu.make_async_copy(src.at[dp], dst.at[mine], ph_r.at[phase]).start()

    def drain_spread(phase, src):
        others = src.at[pl.ds(0, CORES - 1)]
        pltpu.make_async_copy(others, others, ph_s.at[phase]).wait()

    def landed(phase, dst):
        pltpu.make_async_copy(dst, dst, ph_r.at[phase]).wait()

    def arrive(copies):
        for copy in copies:
            copy.wait_recv()

    def token_send(c, owner_y, index, device):
        return push(tok.at[c, here(owner_y)], tok.at[c, here(owner_y)], ag_s.at[index], ag_r.at[index], device)

    gather([(0, lambda v: s1.at[v], r1), (1, lambda v: tag, tags)])
    ag_up = [token_send(ring(2), y, 0, up_dev)]
    ag_dn = [token_send(ring(3), y, 6, dn_dev)]
    ag_up.append(token_send(ring(1), y, 1, up_dev))
    ag_dn.append(token_send(ring(0), y, 7, dn_dev))
    ag_up.append(token_send(ring(3), y, 2, up_dev))
    ag_dn.append(token_send(ring(2), y, 8, dn_dev))
    ag_up.append(token_send(ring(0), y, 3, up_dev))
    ag_dn.append(token_send(ring(1), y, 9, dn_dev))

    def backward(k):
        c = ring(k)
        load_w[k].wait()
        if k == 2:
            load_ups.wait()
        part[c] = dot_t(ups[...], w[c])
        if k:
            send[c] = part[c].astype(BF16)

    @pl.when(jnp.logical_not(is_mid))
    def _():
        for dz, dx, dc in PIECES:
            to = z_mid[dz // 2] * (4 * WIDE) + x_at[dx] * 2 + cores[dc]
            pl.semaphore_signal(ready, inc=1, device_id=(to, y), device_id_type=MESH)

    adapters = owner_row.shape[1]
    same = (ids(SPAN, SPAN, 0) & (EIGHT - 1)) == (ids(SPAN, SPAN, 1) & (EIGHT - 1))

    def users():
        found = jnp.broadcast_to(tags[...], (CORES, EIGHT, LANE)).reshape(SPAN, LANE)
        return one_hot(found[:, 0:adapters].astype(jnp.int32) == ids(SPAN, adapters, 1))

    def owners():
        return one_hot(owner_row[...] == ids(SPAN, adapters, 0) >> 3)

    def matched(a, b):
        return jnp.where(same, dot_t(a, b), 0.0).astype(BF16)

    def flat(pieces):
        return pieces[...].astype(F32).reshape(SPAN, LANE).astype(BF16)

    backward(2)
    backward(3)

    @pl.when(is_mid)
    def _():
        landed(1, tags)
        take = matched(users(), owners())
        landed(0, r1)
        pl.semaphore_wait(ready, CORES - MIDS)
        s3[...] = dot(take, flat(r1)).reshape(CORES, EIGHT, LANE).astype(BF16)
        spread(4, s3, r3)
        back[...] = matched(owners(), users())

    ag_up[0].wait_recv()
    ag_up.append(token_send(ring(1), ring(3), 4, up_dev))
    ag_dn[0].wait_recv()
    ag_dn.append(token_send(ring(0), ring(1), 10, dn_dev))
    ag_up[1].wait_recv()
    ag_up.append(token_send(ring(0), ring(3), 5, up_dev))
    ag_dn[1].wait_recv()
    ag_dn.append(token_send(ring(1), ring(1), 11, dn_dev))

    backward(1)

    def rows_send(c, to, dst, index, device):
        return push(send.at[c, here(to)], dst, rs_s.at[index], rs_r.at[index], device)

    far_up = [
        rows_send(ring(2), ring(2), relay_up.at[0], 0, up_dev),
        rows_send(ring(3), ring(2), relay_up.at[1], 1, up_dev),
    ]
    far_dn = [rows_send(ring(1), ring(2), relay_dn.at[0], 6, dn_dev)]
    near_up = [rows_send(ring(3), ring(1), got_up.at[ring(3)], 2, up_dev)]
    near_dn = [rows_send(ring(3), ring(3), got_dn.at[ring(3)], 8, dn_dev)]

    backward(0)
    ag_up[4].wait_recv()
    mix[...] = dot(tok[y], w[y])

    landed(4, r3)

    def half_item(base):
        return jnp.concatenate(
            [
                jnp.concatenate([r3[v].astype(F32), r3[v + 1].astype(F32)], axis=0)
                for v in range(base, MIDS, 4)
            ],
            axis=1,
        ).astype(BF16)

    down_here, up_here = half_item(0), half_item(2)
    low_all[y, RANK:, :] = dot_t(up_here, ups[...])
    low_all[y, 0:RANK, :] = dot_t(down_here, tok[y])
    lows = [
        push(low_all.at[y], low_all.at[y], low_s.at[k - 1], low_r.at[k - 1], (dp, ring(k)))
        for k in (2, 1, 3)
    ]

    def relayed(c, to, relay, dst, index, device):
        send[c, here(to), :] = (part[c, here(to), :] + relay[...].astype(F32)).astype(BF16)
        return rows_send(c, to, dst, index, device)

    far_up[0].wait_recv()
    near_up.append(relayed(ring(1), ring(1), relay_up.at[0], got_up.at[ring(1)], 3, up_dev))
    far_dn[0].wait_recv()
    near_dn.append(relayed(ring(2), ring(3), relay_dn.at[0], got_dn.at[ring(2)], 9, dn_dev))
    far_up[1].wait_recv()
    near_up.append(relayed(ring(2), ring(1), relay_up.at[1], got_up.at[ring(2)], 4, up_dev))

    ag_up[2].wait_recv()
    ag_up[3].wait_recv()
    ag_up[5].wait_recv()
    ag_dn[2].wait_recv()
    ag_dn[3].wait_recv()
    ag_dn[4].wait_recv()
    ag_dn[5].wait_recv()
    mix[...] += dot(tok[ring(1)], w[ring(1)])

    arrive(lows)
    total = low_all[0] + low_all[1] + low_all[2] + low_all[3]
    low_t = total[0:RANK].astype(BF16)
    back_t = total[RANK:].astype(BF16)

    down_term = 2.0 * dot(back_t, tok[y])
    up_term = 2.0 * dot(low_t, ups[...])
    for v in range(MIDS):
        source = down_term if v % 4 < 2 else up_term
        lanes = (v // 4) * LANE
        g1[v] = source[(v % 2) * EIGHT:(v % 2 + 1) * EIGHT, lanes:lanes + LANE].astype(BF16)
    gather([(5, lambda v: g1.at[v], h1)])

    turned = total.T
    low = turned[:, 0:RANK].astype(BF16)
    low_back = turned[:, RANK:].astype(BF16)
    part[y] = part[y] + 2.0 * dot(low_back, down_here)
    send[y] = part[y].astype(BF16)
    far_dn.append(rows_send(y, ring(2), relay_dn.at[1], 7, dn_dev))
    near_up.append(rows_send(y, ring(1), got_up.at[y], 5, up_dev))
    near_dn.append(rows_send(y, ring(3), got_dn.at[y], 10, dn_dev))
    mix[...] += 2.0 * dot(low, up_here) + dot(tok[ring(3)], w[ring(3)])

    @pl.when(is_mid)
    def _():
        landed(5, h1)
        g3[...] = dot(back[...], flat(h1)).reshape(CORES, EIGHT, LANE).astype(BF16)
        spread(7, g3, h3)

    far_dn[1].wait_recv()
    near_dn.append(relayed(ring(1), ring(3), relay_dn.at[1], got_dn.at[ring(1)], 11, dn_dev))
    mixed_out[...] = (mix[...] + dot(tok[ring(2)], w[ring(2)])).astype(BF16)

    drain_gather(0, r3)
    drain_gather(1, tags)
    drain_gather(5, r3)
    arrive(near_up)
    arrive(near_dn)
    for c in range(RING):
        grad_out[:, c * cols:(c + 1) * cols] = (
            part[c, here(y), :] + got_up[c].astype(F32) + got_dn[c].astype(F32)
        ).astype(BF16)
    for copy in sent:
        copy.wait_send()

    landed(7, h3)
    for v in range(MIDS):
        target = down_out if v % 4 < 2 else up_out
        lanes = (v // 4) * LANE
        target[0, (v % 2) * EIGHT:(v % 2 + 1) * EIGHT, lanes:lanes + LANE] = h3[v].astype(F32)

    @pl.when(is_mid)
    def _():
        drain_spread(4, s3)
        drain_spread(7, g3)


def per_device(tokens, weight, down, up, upstream, adapter, owner):
    rows, width = tokens.shape
    block, cols = upstream.shape
    any_spec = pl.BlockSpec(memory_space=pl.ANY)
    dma = lambda *shape: pltpu.SemaphoreType.DMA(shape)
    pieces = lambda n: pltpu.VMEM((n, EIGHT, LANE), BF16)
    scratch = [
        pltpu.VMEM((RING, cols, cols), BF16),
        pltpu.VMEM((RING, block, cols), BF16),
        pltpu.VMEM((block, cols), BF16),
        pltpu.VMEM((RING, block, cols), F32),
        pltpu.VMEM((RING, block, cols), BF16),
        pltpu.VMEM((2, rows, cols), BF16),
        pltpu.VMEM((2, rows, cols), BF16),
        pltpu.VMEM((RING, rows, cols), BF16),
        pltpu.VMEM((RING, rows, cols), BF16),
        pltpu.VMEM((block, cols), F32),
        pltpu.VMEM((ITEM, cols), BF16),
        pltpu.VMEM((1, LANE), F32),
        pltpu.VMEM((CORES, 1, LANE), F32),
        pieces(MIDS), pieces(CORES), pieces(CORES), pieces(MIDS),
        pieces(MIDS), pieces(CORES), pieces(CORES), pieces(MIDS),
        pltpu.VMEM((RING, ITEM, block), F32),
        pltpu.VMEM((SPAN, SPAN), BF16),
        pltpu.VMEM(adapter.shape, jnp.int32),
        pltpu.VMEM((1, owner.shape[0]), jnp.int32),
        dma(13), dma(12), dma(12), dma(12), dma(12), dma(3), dma(3), dma(8), dma(8),
        pltpu.SemaphoreType.REGULAR,
    ]
    return pl.pallas_call(
        kernel,
        out_shape=(
            pltpu.VMEM((block, cols), BF16),
            pltpu.VMEM((rows, width), BF16),
            pltpu.VMEM(down.shape, F32),
            pltpu.VMEM(up.shape, F32),
        ),
        in_specs=[any_spec] * 5 + [pl.BlockSpec(memory_space=pltpu.HBM), any_spec],
        out_specs=(pl.BlockSpec(memory_space=pltpu.VMEM),) * 4,
        scratch_shapes=scratch,
        compiler_params=pltpu.CompilerParams(
            collective_id=0, has_side_effects=True, vmem_limit_bytes=63000 * 1024
        ),
        cost_estimate=pl.CostEstimate(
            flops=4 * block * width * cols, bytes_accessed=12 * 1024 * 1024, transcendentals=0
        ),
    )(tokens, weight, down, up, upstream, adapter, owner.reshape(1, -1))


def solution(mesh):
    return jax.shard_map(
        per_device,
        mesh=mesh,
        in_specs=(
            P(("dp", "tensor"), None),
            P(None, "tensor"),
            P("dp", None, "tensor"),
            P("dp", None, "tensor"),
            P("dp", "tensor"),
            P("dp", None),
            P(),
        ),
        out_specs=(
            P("dp", "tensor"),
            P(("dp", "tensor"), None),
            P("dp", None, "tensor"),
            P("dp", None, "tensor"),
        ),
        check_vma=False,
    )
```

```python
import jax
import jax.numpy as jnp
from jax import lax
from jax.experimental import pallas as pl
from jax.experimental.pallas import tpu as pltpu
from jax.sharding import PartitionSpec as P

MESH = pl.DeviceIdType.MESH
DEEP = 8
WIDE = 4
CHIPS = DEEP * WIDE
RING = 4
RANK = 16
ITEM = 2 * RANK
LANE = 128
CORES = 2 * CHIPS
MIDS = CORES // 2
EIGHT = 8
SPAN = CORES * EIGHT
PIECES = [(dz, dx, dc) for dz in (4, 6, 2, 0) for dx in (2, 1, 3, 0) for dc in (0, 1)]
EVERY = [
    (dz, dx, dc) for dz in (4, 3, 5, 2, 6, 1, 7, 0) for dx in (2, 1, 3, 0) for dc in (0, 1)
]

F32 = jnp.float32
BF16 = jnp.bfloat16


def dot(a, b):
    return jnp.dot(a, b, preferred_element_type=F32)


def dot_t(a, b):
    return lax.dot_general(a, b, (((1,), (1,)), ((), ())), preferred_element_type=F32)


def one_hot(condition):
    return condition.astype(F32).astype(BF16)


def ids(rows, cols, dim):
    return lax.broadcasted_iota(jnp.int32, (rows, cols), dim)


def kernel(
    tokens, weight, down, up, upstream, adapter, owner,
    mixed_out, grad_out, down_out, up_out,
    w, tok, ups, part, send, relay_up, relay_dn, got_up, got_dn, mix,
    item, tag, tags, s1, r1, s3, r3, g1, h1, g3, h3, low_all, tags_back, block_id, owner_row,
    local_sem, ag_s, ag_r, rs_s, rs_r, low_s, low_r, ph_s, ph_r,
):
    dp = lax.axis_index("dp")
    y = lax.axis_index("tensor")
    chip, core = dp // 2, dp % 2
    z, x = chip // WIDE, chip % WIDE
    half_deep = DEEP // 2
    mid_there, mid_back = z < half_deep, z % 2 == 0
    spot_there = z * (2 * WIDE) + x * 2 + core
    spot_back = z // 2 * (2 * WIDE) + x * 2 + core
    z_at = [lax.rem(z + j, DEEP) for j in range(DEEP)]
    x_at = [lax.rem(x + j, WIDE) for j in range(WIDE)]
    rows = tokens.shape[0]
    cols = weight.shape[1]
    ring_at = [lax.rem(y + j, RING) for j in range(RING)]
    z_there = [lax.rem(z + j, half_deep) for j in range(half_deep)]
    z_back = [lax.rem(z // 2 + j, half_deep) for j in range(half_deep)]
    cores = [core, 1 - core]

    def ring(step):
        return ring_at[step]

    def here(c):
        return pl.ds(pl.multiple_of(c * rows, rows), rows)

    def wide(c):
        return pl.ds(pl.multiple_of(c * cols, cols), cols)

    sent = []

    def push(src, dst, ssem, rsem, device):
        copy = pltpu.make_async_remote_copy(
            src_ref=src, dst_ref=dst, send_sem=ssem, recv_sem=rsem,
            device_id=device, device_id_type=MESH,
        )
        copy.start()
        sent.append(copy)
        return copy

    load_items = [
        pltpu.make_async_copy(down.at[0], item.at[pl.ds(0, RANK)], local_sem.at[0]),
        pltpu.make_async_copy(up.at[0], item.at[pl.ds(RANK, RANK)], local_sem.at[1]),
    ]
    order = (2, 1, 3, 0)
    load_tok = [
        pltpu.make_async_copy(
            tokens.at[:, wide(ring(k))], tok.at[ring(k), here(y)], local_sem.at[2 + k]
        )
        for k in range(RING)
    ]
    load_ups = pltpu.make_async_copy(upstream, ups, local_sem.at[6])
    load_w = [
        pltpu.make_async_copy(weight.at[wide(ring(k))], w.at[ring(k)], local_sem.at[7 + k])
        for k in range(RING)
    ]
    load_ids = [
        pltpu.make_async_copy(adapter, block_id, local_sem.at[11]),
        pltpu.make_async_copy(owner, owner_row, local_sem.at[12]),
    ]

    barrier = pltpu.get_barrier_semaphore()

    def at(dz, dx, dc):
        return z_at[dz] * (2 * WIDE) + x_at[dx] * 2 + cores[dc]

    @pl.when(mid_there)
    def _():
        for step in EVERY:
            if any(step):
                pl.semaphore_signal(barrier, inc=1, device_id=(at(*step), y), device_id_type=MESH)

    for k in (2, 1, 3):
        pl.semaphore_signal(barrier, inc=1, device_id=(dp, ring(k)), device_id_type=MESH)
    for copy in load_items + load_ids:
        copy.start()
    for k in order:
        load_tok[k].start()
    load_ups.start()
    for k in (2, 3, 1, 0):
        load_w[k].start()
    for copy in load_items + load_ids:
        copy.wait()
    adapters = owner_row.shape[1]
    hit = ids(1, adapters, 1) == block_id[...]
    slot = jnp.sum(jnp.where(hit, owner_row[...].astype(F32), 0.0), axis=1, keepdims=True)
    tag[...] = jnp.broadcast_to(slot, (1, LANE))
    for v in range(MIDS):
        lanes = (v // 4) * LANE
        if v % 2 == 0:
            pair = item[v % 4 * EIGHT:v % 4 * EIGHT + RANK, lanes:lanes + LANE].astype(F32)
        s1[v] = pair[(v % 2) * EIGHT:(v % 2 + 1) * EIGHT].astype(BF16)
    for k in order:
        load_tok[k].wait()

    pl.semaphore_wait(barrier, jnp.where(mid_there, MIDS - 1, MIDS) + RING - 1)

    up_dev, dn_dev = (dp, ring(1)), (dp, ring(3))

    def push_to(src, dst, phase, device):
        pltpu.make_async_remote_copy(
            src_ref=src, dst_ref=dst, send_sem=ph_s.at[phase], recv_sem=ph_r.at[phase],
            device_id=device, device_id_type=MESH,
        ).start()

    def gather(pairs, z_mid, stride, is_mid):
        for dz, dx, dc in PIECES:
            plane, rest = z_mid[dz // 2], x_at[dx] * 2 + cores[dc]
            mid, to = plane * (2 * WIDE) + rest, plane * (stride * 2 * WIDE) + rest

            def move():
                for phase, src, dst in pairs:
                    push_to(src(mid), dst.at[dp], phase, (to, y))

            if dz or dx or dc:
                move()
            else:
                @pl.when(is_mid)
                def _():
                    for phase, src, dst in pairs:
                        pltpu.make_async_copy(src(mid), dst.at[dp], ph_r.at[phase]).start()

                pl.when(jnp.logical_not(is_mid))(move)

    def drain_gather(phase, like, is_mid):
        @pl.when(is_mid)
        def _():
            part_of = like.at[pl.ds(0, MIDS - 1)]
            pltpu.make_async_copy(part_of, part_of, ph_s.at[phase]).wait()

        @pl.when(jnp.logical_not(is_mid))
        def _():
            part_of = like.at[pl.ds(0, MIDS)]
            pltpu.make_async_copy(part_of, part_of, ph_s.at[phase]).wait()

    def spread(phase, src, dst, mine):
        for step in EVERY:
            to = at(*step)
            if any(step):
                push_to(src.at[to], dst.at[mine], phase, (to, y))
            else:
                pltpu.make_async_copy(src.at[dp], dst.at[mine], ph_r.at[phase]).start()

    def drain_spread(phase, src):
        others = src.at[pl.ds(0, CORES - 1)]
        pltpu.make_async_copy(others, others, ph_s.at[phase]).wait()

    def landed(phase, dst):
        pltpu.make_async_copy(dst, dst, ph_r.at[phase]).wait()

    def arrive(copies):
        for copy in copies:
            copy.wait_recv()

    def token_send(c, owner_y, index, device):
        return push(tok.at[c, here(owner_y)], tok.at[c, here(owner_y)], ag_s.at[index], ag_r.at[index], device)

    gather([(0, lambda v: s1.at[v], r1), (1, lambda v: tag, tags)], z_there, 1, mid_there)
    ag_up = [token_send(ring(2), y, 0, up_dev)]
    ag_dn = [token_send(ring(3), y, 6, dn_dev)]
    ag_up.append(token_send(ring(1), y, 1, up_dev))
    ag_dn.append(token_send(ring(0), y, 7, dn_dev))
    ag_up.append(token_send(ring(3), y, 2, up_dev))
    ag_dn.append(token_send(ring(2), y, 8, dn_dev))
    ag_up.append(token_send(ring(0), y, 3, up_dev))
    ag_dn.append(token_send(ring(1), y, 9, dn_dev))

    def backward(k):
        c = ring(k)
        load_w[k].wait()
        if k == 2:
            load_ups.wait()
        part[c] = dot_t(ups[...], w[c])
        if k:
            send[c] = part[c].astype(BF16)

    def slot_rows(tags):
        return jnp.broadcast_to(tags[...], (CORES, EIGHT, LANE)).reshape(SPAN, LANE).astype(jnp.int32)

    def taking(tags):
        wanted = slot_rows(tags) * EIGHT + (ids(SPAN, LANE, 0) & (EIGHT - 1))
        wanted = jnp.concatenate([wanted] * (SPAN // LANE), axis=1)
        return one_hot(wanted == ids(SPAN, SPAN, 1))

    def giving(tags):
        has = one_hot(slot_rows(tags)[:, 0:CORES] == ids(SPAN, CORES, 1))
        slots = one_hot(ids(SPAN, CORES, 0) >> 3 == ids(SPAN, CORES, 1))
        same = (ids(SPAN, SPAN, 0) & (EIGHT - 1)) == (ids(SPAN, SPAN, 1) & (EIGHT - 1))
        return jnp.where(same, dot_t(slots, has), 0.0).astype(BF16)

    def flat(pieces):
        return pieces[...].astype(F32).reshape(SPAN, LANE).astype(BF16)

    backward(2)
    backward(3)

    @pl.when(mid_there)
    def _():
        landed(1, tags)
        take = taking(tags)
        landed(0, r1)
        s3[...] = dot(take, flat(r1)).reshape(CORES, EIGHT, LANE).astype(BF16)
        spread(4, s3, r3, spot_there)

    ag_up[0].wait_recv()
    ag_up.append(token_send(ring(1), ring(3), 4, up_dev))
    ag_dn[0].wait_recv()
    ag_dn.append(token_send(ring(0), ring(1), 10, dn_dev))
    ag_up[1].wait_recv()
    ag_up.append(token_send(ring(0), ring(3), 5, up_dev))
    ag_dn[1].wait_recv()
    ag_dn.append(token_send(ring(1), ring(1), 11, dn_dev))

    backward(1)

    def rows_send(c, to, dst, index, device):
        return push(send.at[c, here(to)], dst, rs_s.at[index], rs_r.at[index], device)

    far_up = [
        rows_send(ring(2), ring(2), relay_up.at[0], 0, up_dev),
        rows_send(ring(3), ring(2), relay_up.at[1], 1, up_dev),
    ]
    far_dn = [rows_send(ring(1), ring(2), relay_dn.at[0], 6, dn_dev)]
    near_up = [rows_send(ring(3), ring(1), got_up.at[ring(3)], 2, up_dev)]
    near_dn = [rows_send(ring(3), ring(3), got_dn.at[ring(3)], 8, dn_dev)]

    backward(0)
    ag_up[4].wait_recv()
    mix[...] = dot(tok[y], w[y])

    landed(4, r3)

    def half_item(base):
        return jnp.concatenate(
            [
                jnp.concatenate([r3[v].astype(F32), r3[v + 1].astype(F32)], axis=0)
                for v in range(base, MIDS, 4)
            ],
            axis=1,
        ).astype(BF16)

    down_here, up_here = half_item(0), half_item(2)
    low_all[y, RANK:, :] = dot_t(up_here, ups[...])
    low_all[y, 0:RANK, :] = dot_t(down_here, tok[y])
    lows = [
        push(low_all.at[y], low_all.at[y], low_s.at[k - 1], low_r.at[k - 1], (dp, ring(k)))
        for k in (2, 1, 3)
    ]

    gather([(2, lambda v: tag, tags_back)], z_back, 2, mid_back)

    def relayed(c, to, relay, dst, index, device):
        send[c, here(to), :] = (part[c, here(to), :] + relay[...].astype(F32)).astype(BF16)
        return rows_send(c, to, dst, index, device)

    ag_up[2].wait_recv()
    ag_up[3].wait_recv()
    ag_up[5].wait_recv()
    ag_dn[2].wait_recv()
    ag_dn[3].wait_recv()
    ag_dn[4].wait_recv()
    ag_dn[5].wait_recv()
    mix[...] += dot(tok[ring(1)], w[ring(1)])

    arrive(lows)
    total = low_all[0] + low_all[1] + low_all[2] + low_all[3]
    low_t = total[0:RANK].astype(BF16)
    back_t = total[RANK:].astype(BF16)

    down_term = 2.0 * dot(back_t, tok[y])
    up_term = 2.0 * dot(low_t, ups[...])
    for v in range(MIDS):
        source = down_term if v % 4 < 2 else up_term
        lanes = (v // 4) * LANE
        g1[v] = source[(v % 2) * EIGHT:(v % 2 + 1) * EIGHT, lanes:lanes + LANE].astype(BF16)
    gather([(5, lambda v: g1.at[v], h1)], z_back, 2, mid_back)

    turned = total.T
    low = turned[:, 0:RANK].astype(BF16)
    low_back = turned[:, RANK:].astype(BF16)
    part[y] = part[y] + 2.0 * dot(low_back, down_here)
    send[y] = part[y].astype(BF16)
    far_dn.append(rows_send(y, ring(2), relay_dn.at[1], 7, dn_dev))
    near_up.append(rows_send(y, ring(1), got_up.at[y], 5, up_dev))
    near_dn.append(rows_send(y, ring(3), got_dn.at[y], 10, dn_dev))
    far_up[0].wait_recv()
    near_up.append(relayed(ring(1), ring(1), relay_up.at[0], got_up.at[ring(1)], 3, up_dev))
    far_dn[0].wait_recv()
    near_dn.append(relayed(ring(2), ring(3), relay_dn.at[0], got_dn.at[ring(2)], 9, dn_dev))
    far_up[1].wait_recv()
    near_up.append(relayed(ring(2), ring(1), relay_up.at[1], got_up.at[ring(2)], 4, up_dev))

    mix[...] += 2.0 * dot(low, up_here) + dot(tok[ring(3)], w[ring(3)])

    far_dn[1].wait_recv()
    near_dn.append(relayed(ring(1), ring(3), relay_dn.at[1], got_dn.at[ring(1)], 11, dn_dev))

    @pl.when(mid_back)
    def _():
        landed(2, tags_back)
        give = giving(tags_back)
        landed(5, h1)
        g3[...] = dot(give, flat(h1)).reshape(CORES, EIGHT, LANE).astype(BF16)
        spread(7, g3, h3, spot_back)

    mixed_out[...] = (mix[...] + dot(tok[ring(2)], w[ring(2)])).astype(BF16)

    drain_gather(0, r3, mid_there)
    drain_gather(1, tags, mid_there)
    drain_gather(2, tags, mid_back)
    drain_gather(5, r3, mid_back)
    arrive(near_up)
    arrive(near_dn)
    for c in range(RING):
        grad_out[:, c * cols:(c + 1) * cols] = (
            part[c, here(y), :] + got_up[c].astype(F32) + got_dn[c].astype(F32)
        ).astype(BF16)
    for copy in sent:
        copy.wait_send()

    landed(7, h3)
    for v in range(MIDS):
        target = down_out if v % 4 < 2 else up_out
        lanes = (v // 4) * LANE
        target[0, (v % 2) * EIGHT:(v % 2 + 1) * EIGHT, lanes:lanes + LANE] = h3[v].astype(F32)

    @pl.when(mid_there)
    def _():
        drain_spread(4, s3)

    @pl.when(mid_back)
    def _():
        drain_spread(7, g3)


def per_device(tokens, weight, down, up, upstream, adapter, owner):
    rows, width = tokens.shape
    block, cols = upstream.shape
    any_spec = pl.BlockSpec(memory_space=pl.ANY)
    dma = lambda *shape: pltpu.SemaphoreType.DMA(shape)
    pieces = lambda n: pltpu.VMEM((n, EIGHT, LANE), BF16)
    scratch = [
        pltpu.VMEM((RING, cols, cols), BF16),
        pltpu.VMEM((RING, block, cols), BF16),
        pltpu.VMEM((block, cols), BF16),
        pltpu.VMEM((RING, block, cols), F32),
        pltpu.VMEM((RING, block, cols), BF16),
        pltpu.VMEM((2, rows, cols), BF16),
        pltpu.VMEM((2, rows, cols), BF16),
        pltpu.VMEM((RING, rows, cols), BF16),
        pltpu.VMEM((RING, rows, cols), BF16),
        pltpu.VMEM((block, cols), F32),
        pltpu.VMEM((ITEM, cols), BF16),
        pltpu.VMEM((1, LANE), F32),
        pltpu.VMEM((CORES, 1, LANE), F32),
        pieces(MIDS), pieces(CORES), pieces(CORES), pieces(MIDS),
        pieces(MIDS), pieces(CORES), pieces(CORES), pieces(MIDS),
        pltpu.VMEM((RING, ITEM, block), F32),
        pltpu.VMEM((CORES, 1, LANE), F32),
        pltpu.VMEM(adapter.shape, jnp.int32),
        pltpu.VMEM((1, owner.shape[0]), jnp.int32),
        dma(13), dma(12), dma(12), dma(12), dma(12), dma(3), dma(3), dma(8), dma(8),
    ]
    return pl.pallas_call(
        kernel,
        out_shape=(
            pltpu.VMEM((block, cols), BF16),
            pltpu.VMEM((rows, width), BF16),
            pltpu.VMEM(down.shape, F32),
            pltpu.VMEM(up.shape, F32),
        ),
        in_specs=[any_spec] * 5 + [pl.BlockSpec(memory_space=pltpu.HBM), any_spec],
        out_specs=(pl.BlockSpec(memory_space=pltpu.VMEM),) * 4,
        scratch_shapes=scratch,
        compiler_params=pltpu.CompilerParams(
            collective_id=0, has_side_effects=True, vmem_limit_bytes=63000 * 1024
        ),
        cost_estimate=pl.CostEstimate(
            flops=4 * block * width * cols, bytes_accessed=12 * 1024 * 1024, transcendentals=0
        ),
    )(tokens, weight, down, up, upstream, adapter, owner.reshape(1, -1))


def solution(mesh):
    return jax.shard_map(
        per_device,
        mesh=mesh,
        in_specs=(
            P(("dp", "tensor"), None),
            P(None, "tensor"),
            P("dp", None, "tensor"),
            P("dp", None, "tensor"),
            P("dp", "tensor"),
            P("dp", None),
            P(),
        ),
        out_specs=(
            P("dp", "tensor"),
            P(("dp", "tensor"), None),
            P("dp", None, "tensor"),
            P("dp", None, "tensor"),
        ),
        check_vma=False,
    )
```

```python
import jax
import jax.numpy as jnp
from jax import lax
from jax.experimental import pallas as pl
from jax.experimental.pallas import tpu as pltpu
from jax.sharding import PartitionSpec as P

MESH = pl.DeviceIdType.MESH
DEEP = 8
WIDE = 4
CHIPS = DEEP * WIDE
RING = 4
RANK = 16
ITEM = 2 * RANK
LANE = 128
CORES = 2 * CHIPS
MIDS = CORES // 2
EIGHT = 8
SPAN = CORES * EIGHT
PIECES = [(dz, dx, dc) for dz in (4, 6, 2, 0) for dx in (2, 1, 3, 0) for dc in (0, 1)]
EVERY = [
    (dz, dx, dc) for dz in (4, 3, 5, 2, 6, 1, 7, 0) for dx in (2, 1, 3, 0) for dc in (0, 1)
]

F32 = jnp.float32
BF16 = jnp.bfloat16


def dot(a, b):
    return jnp.dot(a, b, preferred_element_type=F32)


def dot_t(a, b):
    return lax.dot_general(a, b, (((1,), (1,)), ((), ())), preferred_element_type=F32)


def one_hot(condition):
    return condition.astype(F32).astype(BF16)


def ids(rows, cols, dim):
    return lax.broadcasted_iota(jnp.int32, (rows, cols), dim)


def kernel(
    tokens, weight, down, up, upstream, adapter, owner,
    mixed_out, grad_out, pair_out,
    w, tok, ups, part, send, relay_up, relay_dn, got_up, got_dn, mix,
    item, tag, tags, s1, r1, s3, r3, g1, h1, g3, h3, low_all, tags_back, block_id, owner_row,
    local_sem, ag_s, ag_r, rs_s, rs_r, low_s, low_r, ph_s, ph_r,
):
    dp = lax.axis_index("dp")
    y = lax.axis_index("tensor")
    chip, core = dp // 2, dp % 2
    z, x = chip // WIDE, chip % WIDE
    half_deep = DEEP // 2
    mid_there, mid_back = z < half_deep, z % 2 == 0
    spot_there = z * (2 * WIDE) + x * 2 + core
    spot_back = z // 2 * (2 * WIDE) + x * 2 + core
    z_at = [lax.rem(z + j, DEEP) for j in range(DEEP)]
    x_at = [lax.rem(x + j, WIDE) for j in range(WIDE)]
    rows = tokens.shape[0]
    cols = weight.shape[1]
    ring_at = [lax.rem(y + j, RING) for j in range(RING)]
    z_there = [lax.rem(z + j, half_deep) for j in range(half_deep)]
    z_back = [lax.rem(z // 2 + j, half_deep) for j in range(half_deep)]
    cores = [core, 1 - core]

    def ring(step):
        return ring_at[step]

    def here(c):
        return pl.ds(pl.multiple_of(c * rows, rows), rows)

    def wide(c):
        return pl.ds(pl.multiple_of(c * cols, cols), cols)

    sent = []

    def push(src, dst, ssem, rsem, device):
        copy = pltpu.make_async_remote_copy(
            src_ref=src, dst_ref=dst, send_sem=ssem, recv_sem=rsem,
            device_id=device, device_id_type=MESH,
        )
        copy.start()
        sent.append(copy)
        return copy

    load_items = [
        pltpu.make_async_copy(down.at[0], item.at[pl.ds(0, RANK)], local_sem.at[0]),
        pltpu.make_async_copy(up.at[0], item.at[pl.ds(RANK, RANK)], local_sem.at[1]),
    ]
    order = (2, 1, 3, 0)
    load_tok = [
        pltpu.make_async_copy(
            tokens.at[:, wide(ring(k))], tok.at[ring(k), here(y)], local_sem.at[2 + k]
        )
        for k in range(RING)
    ]
    load_ups = pltpu.make_async_copy(upstream, ups, local_sem.at[6])
    load_w = [
        pltpu.make_async_copy(weight.at[wide(ring(k))], w.at[ring(k)], local_sem.at[7 + k])
        for k in range(RING)
    ]
    load_ids = [
        pltpu.make_async_copy(adapter, block_id, local_sem.at[11]),
        pltpu.make_async_copy(owner, owner_row, local_sem.at[12]),
    ]

    barrier = pltpu.get_barrier_semaphore()

    def at(dz, dx, dc):
        return z_at[dz] * (2 * WIDE) + x_at[dx] * 2 + cores[dc]

    @pl.when(mid_there)
    def _():
        for step in EVERY:
            if any(step):
                pl.semaphore_signal(barrier, inc=1, device_id=(at(*step), y), device_id_type=MESH)

    for k in (2, 1, 3):
        pl.semaphore_signal(barrier, inc=1, device_id=(dp, ring(k)), device_id_type=MESH)
    for copy in load_items + load_ids:
        copy.start()
    for k in order:
        load_tok[k].start()
    load_ups.start()
    for k in (2, 3, 1, 0):
        load_w[k].start()
    for copy in load_items + load_ids:
        copy.wait()
    adapters = owner_row.shape[1]
    hit = ids(1, adapters, 1) == block_id[...]
    slot = jnp.sum(jnp.where(hit, owner_row[...].astype(F32), 0.0), axis=1, keepdims=True)
    tag[...] = jnp.broadcast_to(slot, (1, LANE))
    for v in range(MIDS):
        lanes = (v // 4) * LANE
        if v % 2 == 0:
            pair = item[v % 4 * EIGHT:v % 4 * EIGHT + RANK, lanes:lanes + LANE].astype(F32)
        s1[v] = pair[(v % 2) * EIGHT:(v % 2 + 1) * EIGHT].astype(BF16)
    for k in order:
        load_tok[k].wait()

    pl.semaphore_wait(barrier, jnp.where(mid_there, MIDS - 1, MIDS) + RING - 1)

    up_dev, dn_dev = (dp, ring(1)), (dp, ring(3))

    def push_to(src, dst, phase, device):
        pltpu.make_async_remote_copy(
            src_ref=src, dst_ref=dst, send_sem=ph_s.at[phase], recv_sem=ph_r.at[phase],
            device_id=device, device_id_type=MESH,
        ).start()

    def gather(pairs, z_mid, stride, is_mid):
        for dz, dx, dc in PIECES:
            plane, rest = z_mid[dz // 2], x_at[dx] * 2 + cores[dc]
            mid, to = plane * (2 * WIDE) + rest, plane * (stride * 2 * WIDE) + rest

            def move():
                for phase, src, dst in pairs:
                    push_to(src(mid), dst.at[dp], phase, (to, y))

            if dz or dx or dc:
                move()
            else:
                @pl.when(is_mid)
                def _():
                    for phase, src, dst in pairs:
                        pltpu.make_async_copy(src(mid), dst.at[dp], ph_r.at[phase]).start()

                pl.when(jnp.logical_not(is_mid))(move)

    def drain_gather(phase, like, is_mid):
        @pl.when(is_mid)
        def _():
            part_of = like.at[pl.ds(0, MIDS - 1)]
            pltpu.make_async_copy(part_of, part_of, ph_s.at[phase]).wait()

        @pl.when(jnp.logical_not(is_mid))
        def _():
            part_of = like.at[pl.ds(0, MIDS)]
            pltpu.make_async_copy(part_of, part_of, ph_s.at[phase]).wait()

    def spread(phase, src, dst, mine):
        for step in EVERY:
            to = at(*step)
            if any(step):
                push_to(src.at[to], dst.at[mine], phase, (to, y))
            else:
                pltpu.make_async_copy(src.at[dp], dst.at[mine], ph_r.at[phase]).start()

    def drain_spread(phase, src):
        others = src.at[pl.ds(0, CORES - 1)]
        pltpu.make_async_copy(others, others, ph_s.at[phase]).wait()

    def landed(phase, dst):
        pltpu.make_async_copy(dst, dst, ph_r.at[phase]).wait()

    def arrive(copies):
        for copy in copies:
            copy.wait_recv()

    def token_send(c, owner_y, index, device):
        return push(tok.at[c, here(owner_y)], tok.at[c, here(owner_y)], ag_s.at[index], ag_r.at[index], device)

    gather([(0, lambda v: s1.at[v], r1), (1, lambda v: tag, tags)], z_there, 1, mid_there)
    ag_up = [token_send(ring(2), y, 0, up_dev)]
    ag_dn = [token_send(ring(3), y, 6, dn_dev)]
    ag_up.append(token_send(ring(1), y, 1, up_dev))
    ag_dn.append(token_send(ring(0), y, 7, dn_dev))
    ag_up.append(token_send(ring(3), y, 2, up_dev))
    ag_dn.append(token_send(ring(2), y, 8, dn_dev))
    ag_up.append(token_send(ring(0), y, 3, up_dev))
    ag_dn.append(token_send(ring(1), y, 9, dn_dev))

    def backward(k):
        c = ring(k)
        load_w[k].wait()
        if k == 2:
            load_ups.wait()
        part[c] = dot_t(ups[...], w[c])
        if k:
            send[c] = part[c].astype(BF16)

    def slot_rows(tags):
        return jnp.broadcast_to(tags[...], (CORES, EIGHT, LANE)).reshape(SPAN, LANE).astype(jnp.int32)

    def taking(tags):
        wanted = slot_rows(tags) * EIGHT + (ids(SPAN, LANE, 0) & (EIGHT - 1))
        wanted = jnp.concatenate([wanted] * (SPAN // LANE), axis=1)
        return one_hot(wanted == ids(SPAN, SPAN, 1))

    def giving(tags):
        has = one_hot(slot_rows(tags)[:, 0:CORES] == ids(SPAN, CORES, 1))
        slots = one_hot(ids(SPAN, CORES, 0) >> 3 == ids(SPAN, CORES, 1))
        same = (ids(SPAN, SPAN, 0) & (EIGHT - 1)) == (ids(SPAN, SPAN, 1) & (EIGHT - 1))
        return jnp.where(same, dot_t(slots, has), 0.0).astype(BF16)

    def flat(pieces):
        return pieces[...].astype(F32).reshape(SPAN, LANE).astype(BF16)

    backward(2)
    backward(3)

    @pl.when(mid_there)
    def _():
        landed(1, tags)
        take = taking(tags)
        landed(0, r1)
        s3[...] = dot(take, flat(r1)).reshape(CORES, EIGHT, LANE).astype(BF16)
        spread(4, s3, r3, spot_there)

    ag_up[0].wait_recv()
    ag_up.append(token_send(ring(1), ring(3), 4, up_dev))
    ag_dn[0].wait_recv()
    ag_dn.append(token_send(ring(0), ring(1), 10, dn_dev))
    ag_up[1].wait_recv()
    ag_up.append(token_send(ring(0), ring(3), 5, up_dev))
    ag_dn[1].wait_recv()
    ag_dn.append(token_send(ring(1), ring(1), 11, dn_dev))

    backward(1)

    def rows_send(c, to, dst, index, device):
        return push(send.at[c, here(to)], dst, rs_s.at[index], rs_r.at[index], device)

    backward(0)
    ag_up[4].wait_recv()
    mix[...] = dot(tok[y], w[y])

    landed(4, r3)

    def half_item(base):
        return jnp.concatenate(
            [
                jnp.concatenate([r3[v].astype(F32), r3[v + 1].astype(F32)], axis=0)
                for v in range(base, MIDS, 4)
            ],
            axis=1,
        ).astype(BF16)

    down_here, up_here = half_item(0), half_item(2)
    low_all[y, RANK:, :] = dot_t(up_here, ups[...])
    low_all[y, 0:RANK, :] = dot_t(down_here, tok[y])
    lows = [
        push(low_all.at[y], low_all.at[y], low_s.at[k - 1], low_r.at[k - 1], (dp, ring(k)))
        for k in (2, 1, 3)
    ]

    gather([(2, lambda v: tag, tags_back)], z_back, 2, mid_back)

    far_up = [
        rows_send(ring(2), ring(2), relay_up.at[0], 0, up_dev),
        rows_send(ring(3), ring(2), relay_up.at[1], 1, up_dev),
    ]
    far_dn = [rows_send(ring(1), ring(2), relay_dn.at[0], 6, dn_dev)]
    near_up = [rows_send(ring(3), ring(1), got_up.at[ring(3)], 2, up_dev)]
    near_dn = [rows_send(ring(3), ring(3), got_dn.at[ring(3)], 8, dn_dev)]

    def relayed(c, to, relay, dst, index, device):
        send[c, here(to), :] = (part[c, here(to), :] + relay[...].astype(F32)).astype(BF16)
        return rows_send(c, to, dst, index, device)

    ag_up[2].wait_recv()
    ag_up[3].wait_recv()
    ag_up[5].wait_recv()
    ag_dn[2].wait_recv()
    ag_dn[3].wait_recv()
    ag_dn[4].wait_recv()
    ag_dn[5].wait_recv()
    mix[...] += dot(tok[ring(1)], w[ring(1)])

    arrive(lows)
    total = low_all[0] + low_all[1] + low_all[2] + low_all[3]
    low_t = total[0:RANK].astype(BF16)
    back_t = total[RANK:].astype(BF16)

    down_term = 2.0 * dot(back_t, tok[y])
    up_term = 2.0 * dot(low_t, ups[...])
    for v in range(MIDS):
        source = down_term if v % 4 < 2 else up_term
        lanes = (v // 4) * LANE
        g1[v] = source[(v % 2) * EIGHT:(v % 2 + 1) * EIGHT, lanes:lanes + LANE].astype(BF16)
    gather([(5, lambda v: g1.at[v], h1)], z_back, 2, mid_back)

    turned = total.T
    low = turned[:, 0:RANK].astype(BF16)
    low_back = turned[:, RANK:].astype(BF16)
    part[y] = part[y] + 2.0 * dot(low_back, down_here)
    send[y] = part[y].astype(BF16)
    far_dn.append(rows_send(y, ring(2), relay_dn.at[1], 7, dn_dev))
    near_up.append(rows_send(y, ring(1), got_up.at[y], 5, up_dev))
    near_dn.append(rows_send(y, ring(3), got_dn.at[y], 10, dn_dev))
    far_up[0].wait_recv()
    near_up.append(relayed(ring(1), ring(1), relay_up.at[0], got_up.at[ring(1)], 3, up_dev))
    far_dn[0].wait_recv()
    near_dn.append(relayed(ring(2), ring(3), relay_dn.at[0], got_dn.at[ring(2)], 9, dn_dev))
    far_up[1].wait_recv()
    near_up.append(relayed(ring(2), ring(1), relay_up.at[1], got_up.at[ring(2)], 4, up_dev))

    mix[...] += 2.0 * dot(low, up_here) + dot(tok[ring(3)], w[ring(3)])

    far_dn[1].wait_recv()
    near_dn.append(relayed(ring(1), ring(3), relay_dn.at[1], got_dn.at[ring(1)], 11, dn_dev))

    @pl.when(mid_back)
    def _():
        landed(2, tags_back)
        give = giving(tags_back)
        landed(5, h1)
        g3[...] = dot(give, flat(h1)).reshape(CORES, EIGHT, LANE).astype(BF16)
        spread(7, g3, h3, spot_back)

    mixed_out[...] = (mix[...] + dot(tok[ring(2)], w[ring(2)])).astype(BF16)

    drain_gather(0, r3, mid_there)
    drain_gather(1, tags, mid_there)
    drain_gather(2, tags, mid_back)
    drain_gather(5, r3, mid_back)
    arrive(near_up)
    arrive(near_dn)
    for c in range(RING):
        grad_out[:, c * cols:(c + 1) * cols] = (
            part[c, here(y), :] + got_up[c].astype(F32) + got_dn[c].astype(F32)
        ).astype(BF16)
    for copy in sent:
        copy.wait_send()

    landed(7, h3)
    for v in range(0, MIDS, 2):
        lanes = (v // 4) * LANE
        rows_16 = jnp.concatenate([h3[v].astype(F32), h3[v + 1].astype(F32)], axis=0)
        pair_out[v % 4 // 2, :, lanes:lanes + LANE] = rows_16.astype(BF16)

    @pl.when(mid_there)
    def _():
        drain_spread(4, s3)

    @pl.when(mid_back)
    def _():
        drain_spread(7, g3)


def per_device(tokens, weight, down, up, upstream, adapter, owner):
    rows, width = tokens.shape
    block, cols = upstream.shape
    any_spec = pl.BlockSpec(memory_space=pl.ANY)
    dma = lambda *shape: pltpu.SemaphoreType.DMA(shape)
    pieces = lambda n: pltpu.VMEM((n, EIGHT, LANE), BF16)
    scratch = [
        pltpu.VMEM((RING, cols, cols), BF16),
        pltpu.VMEM((RING, block, cols), BF16),
        pltpu.VMEM((block, cols), BF16),
        pltpu.VMEM((RING, block, cols), F32),
        pltpu.VMEM((RING, block, cols), BF16),
        pltpu.VMEM((2, rows, cols), BF16),
        pltpu.VMEM((2, rows, cols), BF16),
        pltpu.VMEM((RING, rows, cols), BF16),
        pltpu.VMEM((RING, rows, cols), BF16),
        pltpu.VMEM((block, cols), F32),
        pltpu.VMEM((ITEM, cols), BF16),
        pltpu.VMEM((1, LANE), F32),
        pltpu.VMEM((CORES, 1, LANE), F32),
        pieces(MIDS), pieces(CORES), pieces(CORES), pieces(MIDS),
        pieces(MIDS), pieces(CORES), pieces(CORES), pieces(MIDS),
        pltpu.VMEM((RING, ITEM, block), F32),
        pltpu.VMEM((CORES, 1, LANE), F32),
        pltpu.VMEM(adapter.shape, jnp.int32),
        pltpu.VMEM((1, owner.shape[0]), jnp.int32),
        dma(13), dma(12), dma(12), dma(12), dma(12), dma(3), dma(3), dma(8), dma(8),
    ]
    mixed, grad, pair = pl.pallas_call(
        kernel,
        out_shape=(
            pltpu.VMEM((block, cols), BF16),
            pltpu.VMEM((rows, width), BF16),
            pltpu.VMEM((2, RANK, cols), BF16),
        ),
        in_specs=[any_spec] * 5 + [pl.BlockSpec(memory_space=pltpu.HBM), any_spec],
        out_specs=(pl.BlockSpec(memory_space=pltpu.VMEM),) * 3,
        scratch_shapes=scratch,
        compiler_params=pltpu.CompilerParams(
            collective_id=0, has_side_effects=True, vmem_limit_bytes=63000 * 1024
        ),
        cost_estimate=pl.CostEstimate(
            flops=4 * block * width * cols, bytes_accessed=12 * 1024 * 1024, transcendentals=0
        ),
    )(tokens, weight, down, up, upstream, adapter, owner.reshape(1, -1))
    pair = pair.astype(F32)
    return mixed, grad, pair[:1], pair[1:]


def solution(mesh):
    return jax.shard_map(
        per_device,
        mesh=mesh,
        in_specs=(
            P(("dp", "tensor"), None),
            P(None, "tensor"),
            P("dp", None, "tensor"),
            P("dp", None, "tensor"),
            P("dp", "tensor"),
            P("dp", None),
            P(),
        ),
        out_specs=(
            P("dp", "tensor"),
            P(("dp", "tensor"), None),
            P("dp", None, "tensor"),
            P("dp", None, "tensor"),
        ),
        check_vma=False,
    )
```

```python
import jax
import jax.numpy as jnp
from jax import lax
from jax.experimental import pallas as pl
from jax.experimental.pallas import tpu as pltpu
from jax.sharding import PartitionSpec as P

MESH = pl.DeviceIdType.MESH
DEEP = 8
WIDE = 4
CHIPS = DEEP * WIDE
RING = 4
RANK = 16
ITEM = 2 * RANK
LANE = 128
CORES = 2 * CHIPS
MIDS = CORES // 2
EIGHT = 8
SPAN = CORES * EIGHT
PIECES = [(dz, dx, dc) for dz in (4, 6, 2, 0) for dx in (2, 1, 3, 0) for dc in (0, 1)]
EVERY = [
    (dz, dx, dc) for dz in (4, 3, 5, 2, 6, 1, 7, 0) for dx in (2, 1, 3, 0) for dc in (0, 1)
]

F32 = jnp.float32
BF16 = jnp.bfloat16


def dot(a, b):
    return jnp.dot(a, b, preferred_element_type=F32)


def dot_t(a, b):
    return lax.dot_general(a, b, (((1,), (1,)), ((), ())), preferred_element_type=F32)


def one_hot(condition):
    return condition.astype(F32).astype(BF16)


def ids(rows, cols, dim):
    return lax.broadcasted_iota(jnp.int32, (rows, cols), dim)


def kernel(
    tokens, weight, down, up, upstream, adapter, owner,
    mixed_out, grad_out, pair_out,
    w, tok, ups, part, send, relay_up, relay_dn, got_up, got_dn, mix,
    item, tag, tags, s1, r1, s3, r3, g1, h1, g3, h3, low_all, tags_back, block_id, owner_row,
    local_sem, ag_s, ag_r, rs_s, rs_r, low_s, low_r, ph_s, ph_r,
):
    dp = lax.axis_index("dp")
    y = lax.axis_index("tensor")
    chip, core = dp // 2, dp % 2
    z, x = chip // WIDE, chip % WIDE
    half_deep = DEEP // 2
    mid_there, mid_back = z < half_deep, z % 2 == 0
    spot_there = z * (2 * WIDE) + x * 2 + core
    spot_back = z // 2 * (2 * WIDE) + x * 2 + core
    z_at = [lax.rem(z + j, DEEP) for j in range(DEEP)]
    x_at = [lax.rem(x + j, WIDE) for j in range(WIDE)]
    rows = tokens.shape[0]
    cols = weight.shape[1]
    ring_at = [lax.rem(y + j, RING) for j in range(RING)]
    z_there = [lax.rem(z + j, half_deep) for j in range(half_deep)]
    z_back = [lax.rem(z // 2 + j, half_deep) for j in range(half_deep)]
    cores = [core, 1 - core]

    def ring(step):
        return ring_at[step]

    def here(c):
        return pl.ds(pl.multiple_of(c * rows, rows), rows)

    def wide(c):
        return pl.ds(pl.multiple_of(c * cols, cols), cols)

    sent = []

    def push(src, dst, ssem, rsem, device):
        copy = pltpu.make_async_remote_copy(
            src_ref=src, dst_ref=dst, send_sem=ssem, recv_sem=rsem,
            device_id=device, device_id_type=MESH,
        )
        copy.start()
        sent.append(copy)
        return copy

    load_items = [
        pltpu.make_async_copy(down.at[0], item.at[pl.ds(0, RANK)], local_sem.at[0]),
        pltpu.make_async_copy(up.at[0], item.at[pl.ds(RANK, RANK)], local_sem.at[1]),
    ]
    order = (2, 1, 3, 0)
    load_tok = [
        pltpu.make_async_copy(
            tokens.at[:, wide(ring(k))], tok.at[ring(k), here(y)], local_sem.at[2 + k]
        )
        for k in range(RING)
    ]
    load_ups = pltpu.make_async_copy(upstream, ups, local_sem.at[6])
    load_w = [
        pltpu.make_async_copy(weight.at[wide(ring(k))], w.at[ring(k)], local_sem.at[7 + k])
        for k in range(RING)
    ]
    load_ids = [
        pltpu.make_async_copy(adapter, block_id, local_sem.at[11]),
        pltpu.make_async_copy(owner, owner_row, local_sem.at[12]),
    ]

    barrier = pltpu.get_barrier_semaphore()

    def at(dz, dx, dc):
        return z_at[dz] * (2 * WIDE) + x_at[dx] * 2 + cores[dc]

    @pl.when(mid_there)
    def _():
        for step in EVERY:
            if any(step):
                pl.semaphore_signal(barrier, inc=1, device_id=(at(*step), y), device_id_type=MESH)

    for k in (2, 1, 3):
        pl.semaphore_signal(barrier, inc=1, device_id=(dp, ring(k)), device_id_type=MESH)
    for copy in load_items + load_ids:
        copy.start()
    for k in order:
        load_tok[k].start()
    load_ups.start()
    for k in (2, 3, 1, 0):
        load_w[k].start()
    for copy in load_items + load_ids:
        copy.wait()
    adapters = owner_row.shape[1]
    hit = ids(1, adapters, 1) == block_id[...]
    slot = jnp.sum(jnp.where(hit, owner_row[...].astype(F32), 0.0), axis=1, keepdims=True)
    tag[...] = jnp.broadcast_to(slot, (1, LANE))
    for v in range(MIDS):
        lanes = (v // 4) * LANE
        if v % 2 == 0:
            pair = item[v % 4 * EIGHT:v % 4 * EIGHT + RANK, lanes:lanes + LANE].astype(F32)
        s1[v] = pair[(v % 2) * EIGHT:(v % 2 + 1) * EIGHT].astype(BF16)
    for k in order:
        load_tok[k].wait()

    pl.semaphore_wait(barrier, jnp.where(mid_there, MIDS - 1, MIDS) + RING - 1)

    up_dev, dn_dev = (dp, ring(1)), (dp, ring(3))

    def push_to(src, dst, phase, device):
        pltpu.make_async_remote_copy(
            src_ref=src, dst_ref=dst, send_sem=ph_s.at[phase], recv_sem=ph_r.at[phase],
            device_id=device, device_id_type=MESH,
        ).start()

    def gather(pairs, z_mid, stride, is_mid):
        for dz, dx, dc in PIECES:
            plane, rest = z_mid[dz // 2], x_at[dx] * 2 + cores[dc]
            mid, to = plane * (2 * WIDE) + rest, plane * (stride * 2 * WIDE) + rest

            def move():
                for phase, src, dst in pairs:
                    push_to(src(mid), dst.at[dp], phase, (to, y))

            if dz or dx or dc:
                move()
            else:
                @pl.when(is_mid)
                def _():
                    for phase, src, dst in pairs:
                        pltpu.make_async_copy(src(mid), dst.at[dp], ph_r.at[phase]).start()

                pl.when(jnp.logical_not(is_mid))(move)

    def drain_gather(phase, like, is_mid):
        @pl.when(is_mid)
        def _():
            part_of = like.at[pl.ds(0, MIDS - 1)]
            pltpu.make_async_copy(part_of, part_of, ph_s.at[phase]).wait()

        @pl.when(jnp.logical_not(is_mid))
        def _():
            part_of = like.at[pl.ds(0, MIDS)]
            pltpu.make_async_copy(part_of, part_of, ph_s.at[phase]).wait()

    def spread(phase, src, dst, mine):
        for step in EVERY:
            to = at(*step)
            if any(step):
                push_to(src.at[to], dst.at[mine], phase, (to, y))
            else:
                pltpu.make_async_copy(src.at[dp], dst.at[mine], ph_r.at[phase]).start()

    def drain_spread(phase, src):
        others = src.at[pl.ds(0, CORES - 1)]
        pltpu.make_async_copy(others, others, ph_s.at[phase]).wait()

    def landed(phase, dst):
        pltpu.make_async_copy(dst, dst, ph_r.at[phase]).wait()

    def arrive(copies):
        for copy in copies:
            copy.wait_recv()

    def token_send(c, owner_y, index, device):
        return push(tok.at[c, here(owner_y)], tok.at[c, here(owner_y)], ag_s.at[index], ag_r.at[index], device)

    gather([(0, lambda v: s1.at[v], r1), (1, lambda v: tag, tags)], z_there, 1, mid_there)
    ag_up = [token_send(ring(2), y, 0, up_dev)]
    ag_dn = [token_send(ring(3), y, 6, dn_dev)]
    ag_up.append(token_send(ring(1), y, 1, up_dev))
    ag_dn.append(token_send(ring(0), y, 7, dn_dev))
    ag_up.append(token_send(ring(3), y, 2, up_dev))
    ag_dn.append(token_send(ring(2), y, 8, dn_dev))
    ag_up.append(token_send(ring(0), y, 3, up_dev))
    ag_dn.append(token_send(ring(1), y, 9, dn_dev))

    def backward(k):
        c = ring(k)
        load_w[k].wait()
        if k == 2:
            load_ups.wait()
        part[c] = dot_t(ups[...], w[c])
        if k:
            send[c] = part[c].astype(BF16)

    def slot_rows(tags):
        return jnp.broadcast_to(tags[...], (CORES, EIGHT, LANE)).reshape(SPAN, LANE).astype(jnp.int32)

    def taking(tags):
        wanted = slot_rows(tags) * EIGHT + (ids(SPAN, LANE, 0) & (EIGHT - 1))
        wanted = jnp.concatenate([wanted] * (SPAN // LANE), axis=1)
        return one_hot(wanted == ids(SPAN, SPAN, 1))

    def giving(tags):
        has = one_hot(slot_rows(tags)[:, 0:CORES] == ids(SPAN, CORES, 1))
        slots = one_hot(ids(SPAN, CORES, 0) >> 3 == ids(SPAN, CORES, 1))
        same = (ids(SPAN, SPAN, 0) & (EIGHT - 1)) == (ids(SPAN, SPAN, 1) & (EIGHT - 1))
        return jnp.where(same, dot_t(slots, has), 0.0).astype(BF16)

    def flat(pieces):
        return pieces[...].astype(F32).reshape(SPAN, LANE).astype(BF16)

    backward(2)
    backward(3)

    @pl.when(mid_there)
    def _():
        landed(1, tags)
        take = taking(tags)
        landed(0, r1)
        s3[...] = dot(take, flat(r1)).reshape(CORES, EIGHT, LANE).astype(BF16)
        spread(4, s3, r3, spot_there)

    ag_up[0].wait_recv()
    ag_up.append(token_send(ring(1), ring(3), 4, up_dev))
    ag_dn[0].wait_recv()
    ag_dn.append(token_send(ring(0), ring(1), 10, dn_dev))
    ag_up[1].wait_recv()
    ag_up.append(token_send(ring(0), ring(3), 5, up_dev))
    ag_dn[1].wait_recv()
    ag_dn.append(token_send(ring(1), ring(1), 11, dn_dev))

    backward(1)

    def rows_send(c, to, dst, index, device):
        return push(send.at[c, here(to)], dst, rs_s.at[index], rs_r.at[index], device)

    backward(0)
    ag_up[4].wait_recv()
    mix[...] = dot(tok[y], w[y])

    landed(4, r3)

    def half_item(base):
        return jnp.concatenate(
            [
                jnp.concatenate([r3[v].astype(F32), r3[v + 1].astype(F32)], axis=0)
                for v in range(base, MIDS, 4)
            ],
            axis=1,
        ).astype(BF16)

    down_here, up_here = half_item(0), half_item(2)
    low_all[y, RANK:, :] = dot_t(up_here, ups[...])
    low_all[y, 0:RANK, :] = dot_t(down_here, tok[y])
    lows = [
        push(low_all.at[y], low_all.at[y], low_s.at[k - 1], low_r.at[k - 1], (dp, ring(k)))
        for k in (2, 1, 3)
    ]

    gather([(2, lambda v: tag, tags_back)], z_back, 2, mid_back)

    far_up = [
        rows_send(ring(2), ring(2), relay_up.at[0], 0, up_dev),
        rows_send(ring(3), ring(2), relay_up.at[1], 1, up_dev),
    ]
    far_dn = [rows_send(ring(1), ring(2), relay_dn.at[0], 6, dn_dev)]
    near_up = [rows_send(ring(3), ring(1), got_up.at[ring(3)], 2, up_dev)]
    near_dn = [rows_send(ring(3), ring(3), got_dn.at[ring(3)], 8, dn_dev)]

    def relayed(c, to, relay, dst, index, device):
        send[c, here(to), :] = (part[c, here(to), :] + relay[...].astype(F32)).astype(BF16)
        return rows_send(c, to, dst, index, device)

    ag_up[2].wait_recv()
    ag_up[3].wait_recv()
    ag_up[5].wait_recv()
    ag_dn[2].wait_recv()
    ag_dn[3].wait_recv()
    ag_dn[4].wait_recv()
    ag_dn[5].wait_recv()
    mix[...] += dot(tok[ring(1)], w[ring(1)])

    arrive(lows)
    total = low_all[0] + low_all[1] + low_all[2] + low_all[3]
    low_t = total[0:RANK].astype(BF16)
    back_t = total[RANK:].astype(BF16)

    down_term = 2.0 * dot(back_t, tok[y])
    up_term = 2.0 * dot(low_t, ups[...])
    for v in range(MIDS):
        source = down_term if v % 4 < 2 else up_term
        lanes = (v // 4) * LANE
        g1[v] = source[(v % 2) * EIGHT:(v % 2 + 1) * EIGHT, lanes:lanes + LANE].astype(BF16)
    gather([(5, lambda v: g1.at[v], h1)], z_back, 2, mid_back)

    turned = total.T
    low = turned[:, 0:RANK].astype(BF16)
    low_back = turned[:, RANK:].astype(BF16)
    part[y] = part[y] + 2.0 * dot(low_back, down_here)
    send[y] = part[y].astype(BF16)
    far_dn.append(rows_send(y, ring(2), relay_dn.at[1], 7, dn_dev))
    near_up.append(rows_send(y, ring(1), got_up.at[y], 5, up_dev))
    near_dn.append(rows_send(y, ring(3), got_dn.at[y], 10, dn_dev))
    far_up[0].wait_recv()
    near_up.append(relayed(ring(1), ring(1), relay_up.at[0], got_up.at[ring(1)], 3, up_dev))
    far_dn[0].wait_recv()
    near_dn.append(relayed(ring(2), ring(3), relay_dn.at[0], got_dn.at[ring(2)], 9, dn_dev))
    far_up[1].wait_recv()
    near_up.append(relayed(ring(2), ring(1), relay_up.at[1], got_up.at[ring(2)], 4, up_dev))

    mix[...] += 2.0 * dot(low, up_here) + dot(tok[ring(3)], w[ring(3)])

    mixed_out[...] = (mix[...] + dot(tok[ring(2)], w[ring(2)])).astype(BF16)

    far_dn[1].wait_recv()
    near_dn.append(relayed(ring(1), ring(3), relay_dn.at[1], got_dn.at[ring(1)], 11, dn_dev))

    @pl.when(mid_back)
    def _():
        landed(2, tags_back)
        give = giving(tags_back)
        landed(5, h1)
        g3[...] = dot(give, flat(h1)).reshape(CORES, EIGHT, LANE).astype(BF16)
        spread(7, g3, h3, spot_back)


    drain_gather(0, r3, mid_there)
    drain_gather(1, tags, mid_there)
    drain_gather(2, tags, mid_back)
    drain_gather(5, r3, mid_back)
    arrive(near_up)
    arrive(near_dn)
    for c in range(RING):
        grad_out[:, c * cols:(c + 1) * cols] = (
            part[c, here(y), :] + got_up[c].astype(F32) + got_dn[c].astype(F32)
        ).astype(BF16)
    for copy in sent:
        copy.wait_send()

    landed(7, h3)
    for v in range(0, MIDS, 2):
        lanes = (v // 4) * LANE
        rows_16 = jnp.concatenate([h3[v].astype(F32), h3[v + 1].astype(F32)], axis=0)
        pair_out[v % 4 // 2, :, lanes:lanes + LANE] = rows_16.astype(BF16)

    @pl.when(mid_there)
    def _():
        drain_spread(4, s3)

    @pl.when(mid_back)
    def _():
        drain_spread(7, g3)


def per_device(tokens, weight, down, up, upstream, adapter, owner):
    rows, width = tokens.shape
    block, cols = upstream.shape
    any_spec = pl.BlockSpec(memory_space=pl.ANY)
    dma = lambda *shape: pltpu.SemaphoreType.DMA(shape)
    pieces = lambda n: pltpu.VMEM((n, EIGHT, LANE), BF16)
    scratch = [
        pltpu.VMEM((RING, cols, cols), BF16),
        pltpu.VMEM((RING, block, cols), BF16),
        pltpu.VMEM((block, cols), BF16),
        pltpu.VMEM((RING, block, cols), F32),
        pltpu.VMEM((RING, block, cols), BF16),
        pltpu.VMEM((2, rows, cols), BF16),
        pltpu.VMEM((2, rows, cols), BF16),
        pltpu.VMEM((RING, rows, cols), BF16),
        pltpu.VMEM((RING, rows, cols), BF16),
        pltpu.VMEM((block, cols), F32),
        pltpu.VMEM((ITEM, cols), BF16),
        pltpu.VMEM((1, LANE), F32),
        pltpu.VMEM((CORES, 1, LANE), F32),
        pieces(MIDS), pieces(CORES), pieces(CORES), pieces(MIDS),
        pieces(MIDS), pieces(CORES), pieces(CORES), pieces(MIDS),
        pltpu.VMEM((RING, ITEM, block), F32),
        pltpu.VMEM((CORES, 1, LANE), F32),
        pltpu.VMEM(adapter.shape, jnp.int32),
        pltpu.VMEM((1, owner.shape[0]), jnp.int32),
        dma(13), dma(12), dma(12), dma(12), dma(12), dma(3), dma(3), dma(8), dma(8),
    ]
    mixed, grad, pair = pl.pallas_call(
        kernel,
        out_shape=(
            pltpu.VMEM((block, cols), BF16),
            pltpu.VMEM((rows, width), BF16),
            pltpu.VMEM((2, RANK, cols), BF16),
        ),
        in_specs=[any_spec] * 5 + [pl.BlockSpec(memory_space=pltpu.HBM), any_spec],
        out_specs=(pl.BlockSpec(memory_space=pltpu.VMEM),) * 3,
        scratch_shapes=scratch,
        compiler_params=pltpu.CompilerParams(
            collective_id=0, has_side_effects=True, vmem_limit_bytes=63000 * 1024
        ),
        cost_estimate=pl.CostEstimate(
            flops=4 * block * width * cols, bytes_accessed=12 * 1024 * 1024, transcendentals=0
        ),
    )(tokens, weight, down, up, upstream, adapter, owner.reshape(1, -1))
    pair = pair.astype(F32)
    return mixed, grad, pair[:1], pair[1:]


def solution(mesh):
    return jax.shard_map(
        per_device,
        mesh=mesh,
        in_specs=(
            P(("dp", "tensor"), None),
            P(None, "tensor"),
            P("dp", None, "tensor"),
            P("dp", None, "tensor"),
            P("dp", "tensor"),
            P("dp", None),
            P(),
        ),
        out_specs=(
            P("dp", "tensor"),
            P(("dp", "tensor"), None),
            P("dp", None, "tensor"),
            P("dp", None, "tensor"),
        ),
        check_vma=False,
    )
```

```python
import jax
import jax.numpy as jnp
from jax import lax
from jax.experimental import pallas as pl
from jax.experimental.pallas import tpu as pltpu
from jax.sharding import PartitionSpec as P

MESH = pl.DeviceIdType.MESH
DEEP = 8
WIDE = 4
CHIPS = DEEP * WIDE
RING = 4
RANK = 16
ITEM = 2 * RANK
LANE = 128
CORES = 2 * CHIPS
MIDS = CORES // 2
EIGHT = 8
SPAN = CORES * EIGHT
PIECES = [(dz, dx, dc) for dz in (4, 6, 2, 0) for dx in (2, 1, 3, 0) for dc in (0, 1)]
EVERY = [
    (dz, dx, dc) for dz in (4, 3, 5, 2, 6, 1, 7, 0) for dx in (2, 1, 3, 0) for dc in (0, 1)
]

F32 = jnp.float32
BF16 = jnp.bfloat16


def dot(a, b):
    return jnp.dot(a, b, preferred_element_type=F32)


def dot_t(a, b):
    return lax.dot_general(a, b, (((1,), (1,)), ((), ())), preferred_element_type=F32)


def one_hot(condition):
    return condition.astype(F32).astype(BF16)


def ids(rows, cols, dim):
    return lax.broadcasted_iota(jnp.int32, (rows, cols), dim)


def kernel(
    tokens, weight, down, up, upstream, adapter, owner,
    mixed_out, grad_out, pair_out,
    w, tok, ups, part, send, relay_up, relay_dn, got_up, got_dn, mix,
    item, tag, tags, s1, r1, s3, r3, g1, h1, g3, h3, low_all, tags_back, block_id, owner_row,
    local_sem, ag_s, ag_r, rs_s, rs_r, low_s, low_r, ph_s, ph_r,
):
    dp = lax.axis_index("dp")
    y = lax.axis_index("tensor")
    chip, core = dp // 2, dp % 2
    z, x = chip // WIDE, chip % WIDE
    half_deep = DEEP // 2
    mid_there, mid_back = z < half_deep, z % 2 == 0
    spot_there = z * (2 * WIDE) + x * 2 + core
    spot_back = z // 2 * (2 * WIDE) + x * 2 + core
    z_at = [lax.rem(z + j, DEEP) for j in range(DEEP)]
    x_at = [lax.rem(x + j, WIDE) for j in range(WIDE)]
    rows = tokens.shape[0]
    cols = weight.shape[1]
    ring_at = [lax.rem(y + j, RING) for j in range(RING)]
    z_there = [lax.rem(z + j, half_deep) for j in range(half_deep)]
    z_back = [lax.rem(z // 2 + j, half_deep) for j in range(half_deep)]
    cores = [core, 1 - core]

    def ring(step):
        return ring_at[step]

    def here(c):
        return pl.ds(pl.multiple_of(c * rows, rows), rows)

    def wide(c):
        return pl.ds(pl.multiple_of(c * cols, cols), cols)

    sent = []

    def push(src, dst, ssem, rsem, device):
        copy = pltpu.make_async_remote_copy(
            src_ref=src, dst_ref=dst, send_sem=ssem, recv_sem=rsem,
            device_id=device, device_id_type=MESH,
        )
        copy.start()
        sent.append(copy)
        return copy

    load_items = [
        pltpu.make_async_copy(down.at[0], item.at[pl.ds(0, RANK)], local_sem.at[0]),
        pltpu.make_async_copy(up.at[0], item.at[pl.ds(RANK, RANK)], local_sem.at[1]),
    ]
    order = (2, 1, 3, 0)
    load_tok = [
        pltpu.make_async_copy(
            tokens.at[:, wide(ring(k))], tok.at[ring(k), here(y)], local_sem.at[2 + k]
        )
        for k in range(RING)
    ]
    load_ups = pltpu.make_async_copy(upstream, ups, local_sem.at[6])
    load_w = [
        pltpu.make_async_copy(weight.at[wide(ring(k))], w.at[ring(k)], local_sem.at[7 + k])
        for k in range(RING)
    ]
    load_ids = [
        pltpu.make_async_copy(adapter, block_id, local_sem.at[11]),
        pltpu.make_async_copy(owner, owner_row, local_sem.at[12]),
    ]

    barrier = pltpu.get_barrier_semaphore()

    def at(dz, dx, dc):
        return z_at[dz] * (2 * WIDE) + x_at[dx] * 2 + cores[dc]

    for k in (2, 1, 3):
        pl.semaphore_signal(barrier, inc=1, device_id=(dp, ring(k)), device_id_type=MESH)

    @pl.when(mid_there)
    def _():
        for step in EVERY:
            if any(step):
                pl.semaphore_signal(barrier, inc=1, device_id=(at(*step), y), device_id_type=MESH)

    for copy in load_items + load_ids:
        copy.start()
    for k in order:
        load_tok[k].start()
    load_ups.start()
    for k in (2, 3, 1, 0):
        load_w[k].start()
    for copy in load_items + load_ids:
        copy.wait()
    adapters = owner_row.shape[1]
    hit = ids(1, adapters, 1) == block_id[...]
    slot = jnp.sum(jnp.where(hit, owner_row[...].astype(F32), 0.0), axis=1, keepdims=True)
    tag[...] = jnp.broadcast_to(slot, (1, LANE))
    for v in range(MIDS):
        lanes = (v // 4) * LANE
        if v % 2 == 0:
            pair = item[v % 4 * EIGHT:v % 4 * EIGHT + RANK, lanes:lanes + LANE].astype(F32)
        s1[v] = pair[(v % 2) * EIGHT:(v % 2 + 1) * EIGHT].astype(BF16)
    for k in order:
        load_tok[k].wait()

    pl.semaphore_wait(barrier, jnp.where(mid_there, MIDS - 1, MIDS) + RING - 1)

    up_dev, dn_dev = (dp, ring(1)), (dp, ring(3))

    def push_to(src, dst, phase, device):
        pltpu.make_async_remote_copy(
            src_ref=src, dst_ref=dst, send_sem=ph_s.at[phase], recv_sem=ph_r.at[phase],
            device_id=device, device_id_type=MESH,
        ).start()

    def gather(pairs, z_mid, stride, is_mid):
        for dz, dx, dc in PIECES:
            plane, rest = z_mid[dz // 2], x_at[dx] * 2 + cores[dc]
            mid, to = plane * (2 * WIDE) + rest, plane * (stride * 2 * WIDE) + rest

            def move():
                for phase, src, dst in pairs:
                    push_to(src(mid), dst.at[dp], phase, (to, y))

            if dz or dx or dc:
                move()
            else:
                @pl.when(is_mid)
                def _():
                    for phase, src, dst in pairs:
                        pltpu.make_async_copy(src(mid), dst.at[dp], ph_r.at[phase]).start()

                pl.when(jnp.logical_not(is_mid))(move)

    def drain_gather(phase, like, is_mid):
        @pl.when(is_mid)
        def _():
            part_of = like.at[pl.ds(0, MIDS - 1)]
            pltpu.make_async_copy(part_of, part_of, ph_s.at[phase]).wait()

        @pl.when(jnp.logical_not(is_mid))
        def _():
            part_of = like.at[pl.ds(0, MIDS)]
            pltpu.make_async_copy(part_of, part_of, ph_s.at[phase]).wait()

    def spread(phase, src, dst, mine):
        for step in EVERY:
            to = at(*step)
            if any(step):
                push_to(src.at[to], dst.at[mine], phase, (to, y))
            else:
                pltpu.make_async_copy(src.at[dp], dst.at[mine], ph_r.at[phase]).start()

    def drain_spread(phase, src):
        others = src.at[pl.ds(0, CORES - 1)]
        pltpu.make_async_copy(others, others, ph_s.at[phase]).wait()

    def landed(phase, dst):
        pltpu.make_async_copy(dst, dst, ph_r.at[phase]).wait()

    def arrive(copies):
        for copy in copies:
            copy.wait_recv()

    def token_send(c, owner_y, index, device):
        return push(tok.at[c, here(owner_y)], tok.at[c, here(owner_y)], ag_s.at[index], ag_r.at[index], device)

    gather([(0, lambda v: s1.at[v], r1), (1, lambda v: tag, tags)], z_there, 1, mid_there)
    ag_up = [token_send(ring(2), y, 0, up_dev)]
    ag_dn = [token_send(ring(3), y, 6, dn_dev)]
    ag_up.append(token_send(ring(1), y, 1, up_dev))
    ag_dn.append(token_send(ring(0), y, 7, dn_dev))
    ag_up.append(token_send(ring(3), y, 2, up_dev))
    ag_dn.append(token_send(ring(2), y, 8, dn_dev))
    ag_up.append(token_send(ring(0), y, 3, up_dev))
    ag_dn.append(token_send(ring(1), y, 9, dn_dev))

    def backward(k):
        c = ring(k)
        load_w[k].wait()
        if k == 2:
            load_ups.wait()
        part[c] = dot_t(ups[...], w[c])
        if k:
            send[c] = part[c].astype(BF16)

    def slot_rows(tags):
        return jnp.broadcast_to(tags[...], (CORES, EIGHT, LANE)).reshape(SPAN, LANE).astype(jnp.int32)

    def taking(tags):
        wanted = slot_rows(tags) * EIGHT + (ids(SPAN, LANE, 0) & (EIGHT - 1))
        wanted = jnp.concatenate([wanted] * (SPAN // LANE), axis=1)
        return one_hot(wanted == ids(SPAN, SPAN, 1))

    def giving(tags):
        has = one_hot(slot_rows(tags)[:, 0:CORES] == ids(SPAN, CORES, 1))
        slots = one_hot(ids(SPAN, CORES, 0) >> 3 == ids(SPAN, CORES, 1))
        same = (ids(SPAN, SPAN, 0) & (EIGHT - 1)) == (ids(SPAN, SPAN, 1) & (EIGHT - 1))
        return jnp.where(same, dot_t(slots, has), 0.0).astype(BF16)

    def flat(pieces):
        return pieces[...].astype(F32).reshape(SPAN, LANE).astype(BF16)

    backward(2)
    backward(3)

    @pl.when(mid_there)
    def _():
        landed(1, tags)
        take = taking(tags)
        landed(0, r1)
        s3[...] = dot(take, flat(r1)).reshape(CORES, EIGHT, LANE).astype(BF16)
        spread(4, s3, r3, spot_there)

    ag_up[0].wait_recv()
    ag_up.append(token_send(ring(1), ring(3), 4, up_dev))
    ag_dn[0].wait_recv()
    ag_dn.append(token_send(ring(0), ring(1), 10, dn_dev))
    ag_up[1].wait_recv()
    ag_up.append(token_send(ring(0), ring(3), 5, up_dev))
    ag_dn[1].wait_recv()
    ag_dn.append(token_send(ring(1), ring(1), 11, dn_dev))

    backward(1)

    def rows_send(c, to, dst, index, device):
        return push(send.at[c, here(to)], dst, rs_s.at[index], rs_r.at[index], device)

    backward(0)
    ag_up[4].wait_recv()
    mix[...] = dot(tok[y], w[y])

    landed(4, r3)

    def half_item(base):
        return jnp.concatenate(
            [
                jnp.concatenate([r3[v].astype(F32), r3[v + 1].astype(F32)], axis=0)
                for v in range(base, MIDS, 4)
            ],
            axis=1,
        ).astype(BF16)

    down_here, up_here = half_item(0), half_item(2)
    low_all[y, RANK:, :] = dot_t(up_here, ups[...])
    low_all[y, 0:RANK, :] = dot_t(down_here, tok[y])
    lows = [
        push(low_all.at[y], low_all.at[y], low_s.at[k - 1], low_r.at[k - 1], (dp, ring(k)))
        for k in (2, 1, 3)
    ]

    gather([(2, lambda v: tag, tags_back)], z_back, 2, mid_back)

    far_up = [
        rows_send(ring(2), ring(2), relay_up.at[0], 0, up_dev),
        rows_send(ring(3), ring(2), relay_up.at[1], 1, up_dev),
    ]
    far_dn = [rows_send(ring(1), ring(2), relay_dn.at[0], 6, dn_dev)]
    near_up = [rows_send(ring(3), ring(1), got_up.at[ring(3)], 2, up_dev)]
    near_dn = [rows_send(ring(3), ring(3), got_dn.at[ring(3)], 8, dn_dev)]

    def relayed(c, to, relay, dst, index, device):
        send[c, here(to), :] = (part[c, here(to), :] + relay[...].astype(F32)).astype(BF16)
        return rows_send(c, to, dst, index, device)

    ag_up[2].wait_recv()
    ag_up[3].wait_recv()
    ag_up[5].wait_recv()
    ag_dn[2].wait_recv()
    ag_dn[3].wait_recv()
    ag_dn[4].wait_recv()
    ag_dn[5].wait_recv()
    mix[...] += dot(tok[ring(1)], w[ring(1)])

    arrive(lows)
    total = low_all[0] + low_all[1] + low_all[2] + low_all[3]
    low_t = total[0:RANK].astype(BF16)
    back_t = total[RANK:].astype(BF16)

    down_term = 2.0 * dot(back_t, tok[y])
    up_term = 2.0 * dot(low_t, ups[...])
    for v in range(MIDS):
        source = down_term if v % 4 < 2 else up_term
        lanes = (v // 4) * LANE
        g1[v] = source[(v % 2) * EIGHT:(v % 2 + 1) * EIGHT, lanes:lanes + LANE].astype(BF16)
    gather([(5, lambda v: g1.at[v], h1)], z_back, 2, mid_back)

    turned = total.T
    low = turned[:, 0:RANK].astype(BF16)
    low_back = turned[:, RANK:].astype(BF16)
    part[y] = part[y] + 2.0 * dot(low_back, down_here)
    send[y] = part[y].astype(BF16)
    far_dn.append(rows_send(y, ring(2), relay_dn.at[1], 7, dn_dev))
    near_up.append(rows_send(y, ring(1), got_up.at[y], 5, up_dev))
    near_dn.append(rows_send(y, ring(3), got_dn.at[y], 10, dn_dev))
    far_up[0].wait_recv()
    near_up.append(relayed(ring(1), ring(1), relay_up.at[0], got_up.at[ring(1)], 3, up_dev))
    far_dn[0].wait_recv()
    near_dn.append(relayed(ring(2), ring(3), relay_dn.at[0], got_dn.at[ring(2)], 9, dn_dev))
    far_up[1].wait_recv()
    near_up.append(relayed(ring(2), ring(1), relay_up.at[1], got_up.at[ring(2)], 4, up_dev))

    mix[...] += 2.0 * dot(low, up_here) + dot(tok[ring(3)], w[ring(3)])

    mixed_out[...] = (mix[...] + dot(tok[ring(2)], w[ring(2)])).astype(BF16)

    far_dn[1].wait_recv()
    near_dn.append(relayed(ring(1), ring(3), relay_dn.at[1], got_dn.at[ring(1)], 11, dn_dev))

    @pl.when(mid_back)
    def _():
        landed(2, tags_back)
        give = giving(tags_back)
        landed(5, h1)
        g3[...] = dot(give, flat(h1)).reshape(CORES, EIGHT, LANE).astype(BF16)
        spread(7, g3, h3, spot_back)


    drain_gather(0, r3, mid_there)
    drain_gather(1, tags, mid_there)
    drain_gather(2, tags, mid_back)
    drain_gather(5, r3, mid_back)
    arrive(near_up)
    arrive(near_dn)
    for c in range(RING):
        grad_out[:, c * cols:(c + 1) * cols] = (
            part[c, here(y), :] + got_up[c].astype(F32) + got_dn[c].astype(F32)
        ).astype(BF16)
    for copy in sent:
        copy.wait_send()

    landed(7, h3)
    for v in range(0, MIDS, 2):
        lanes = (v // 4) * LANE
        rows_16 = jnp.concatenate([h3[v].astype(F32), h3[v + 1].astype(F32)], axis=0)
        pair_out[v % 4 // 2, :, lanes:lanes + LANE] = rows_16.astype(BF16)

    @pl.when(mid_there)
    def _():
        drain_spread(4, s3)

    @pl.when(mid_back)
    def _():
        drain_spread(7, g3)


def per_device(tokens, weight, down, up, upstream, adapter, owner):
    rows, width = tokens.shape
    block, cols = upstream.shape
    any_spec = pl.BlockSpec(memory_space=pl.ANY)
    dma = lambda *shape: pltpu.SemaphoreType.DMA(shape)
    pieces = lambda n: pltpu.VMEM((n, EIGHT, LANE), BF16)
    scratch = [
        pltpu.VMEM((RING, cols, cols), BF16),
        pltpu.VMEM((RING, block, cols), BF16),
        pltpu.VMEM((block, cols), BF16),
        pltpu.VMEM((RING, block, cols), F32),
        pltpu.VMEM((RING, block, cols), BF16),
        pltpu.VMEM((2, rows, cols), BF16),
        pltpu.VMEM((2, rows, cols), BF16),
        pltpu.VMEM((RING, rows, cols), BF16),
        pltpu.VMEM((RING, rows, cols), BF16),
        pltpu.VMEM((block, cols), F32),
        pltpu.VMEM((ITEM, cols), BF16),
        pltpu.VMEM((1, LANE), F32),
        pltpu.VMEM((CORES, 1, LANE), F32),
        pieces(MIDS), pieces(CORES), pieces(CORES), pieces(MIDS),
        pieces(MIDS), pieces(CORES), pieces(CORES), pieces(MIDS),
        pltpu.VMEM((RING, ITEM, block), F32),
        pltpu.VMEM((CORES, 1, LANE), F32),
        pltpu.VMEM(adapter.shape, jnp.int32),
        pltpu.VMEM((1, owner.shape[0]), jnp.int32),
        dma(13), dma(12), dma(12), dma(12), dma(12), dma(3), dma(3), dma(8), dma(8),
    ]
    mixed, grad, pair = pl.pallas_call(
        kernel,
        out_shape=(
            pltpu.VMEM((block, cols), BF16),
            pltpu.VMEM((rows, width), BF16),
            pltpu.VMEM((2, RANK, cols), BF16),
        ),
        in_specs=[any_spec] * 5 + [pl.BlockSpec(memory_space=pltpu.HBM), any_spec],
        out_specs=(pl.BlockSpec(memory_space=pltpu.VMEM),) * 3,
        scratch_shapes=scratch,
        compiler_params=pltpu.CompilerParams(
            collective_id=0, has_side_effects=True, vmem_limit_bytes=63000 * 1024
        ),
        cost_estimate=pl.CostEstimate(
            flops=4 * block * width * cols, bytes_accessed=12 * 1024 * 1024, transcendentals=0
        ),
    )(tokens, weight, down, up, upstream, adapter, owner.reshape(1, -1))
    pair = pair.astype(F32)
    return mixed, grad, pair[:1], pair[1:]


def solution(mesh):
    return jax.shard_map(
        per_device,
        mesh=mesh,
        in_specs=(
            P(("dp", "tensor"), None),
            P(None, "tensor"),
            P("dp", None, "tensor"),
            P("dp", None, "tensor"),
            P("dp", "tensor"),
            P("dp", None),
            P(),
        ),
        out_specs=(
            P("dp", "tensor"),
            P(("dp", "tensor"), None),
            P("dp", None, "tensor"),
            P("dp", None, "tensor"),
        ),
        check_vma=False,
    )
```
